32 devices in a mesh: set: 8 (over y, x, core), path: 4 (over z).
Axes of the slice: x: 2, y: 2, z: 4, core: 2. Of those that a mesh axis runs over, the one named last changes fastest.
Arguments:
- start_state: float32 [512, 2048], P(('path', 'set')), may hold values from -6 to 6
- shocks: bfloat16 [2, 512, 2048], P(None, ('path', 'set')), may hold values from -6 to 6
- loading: bfloat16 [2048, 2048], replicated, may hold values from -0.125 to 0.125
- decay: float32 [2048], replicated, may hold values from 0.5 to 1
- factor_lists: int32 [1024, 64], P('set'), may hold values from 0 to 2047, all different within a row
- delta: bfloat16 [1024, 64], P('set'), may hold values from -0.75 to 0.75
- gamma: bfloat16 [1024, 64, 64], P('set'), may hold values from -0.09375 to 0.09375
- currency: int32 [1024], P('set'), may hold values from 0 to 15
- owner: int32 [1024], P('set'), may hold values from 0 to 63
Outputs:
- exposure: float32 [2, 64, 512], P(None, 'set', 'path')
- end_state: float32 [512, 2048], P(('path', 'set'))
The draws below stay inside these ranges and needn't reach their ends.
Inputs may be any that keep to these rules, and one draw needn't show every extreme that they name: `factor_lists`: the 64 factors of one netting set are different.
All inputs are finite; a program needn't handle non-finite values.
Results may differ from the reference program's by a relative error of at most 0.004.
Values may be sent and summed in bfloat16 or wider, within the bound.
A program may use at most 64 MiB of HBM per device.

```python
import math
import jax
import jax.numpy as jnp
import numpy as np
from jax import lax

F = 2048
K = 64
NB = 16
NCUR = 16
STEPS = 2
PATHS = 512
SETS = 1024
CPS = 64


def place_ends(drawn, rng, low, high):
    longest = drawn.shape.index(max(drawn.shape))
    spots = []
    for shift in (0, 1):
        where = [jax.random.randint(jax.random.fold_in(rng, axis), (), 0, length) for axis, length in enumerate(drawn.shape)]
        where[longest] = (where[longest] + shift) % drawn.shape[longest]
        spots.append(tuple(where))
    return drawn.at[spots[0]].set(low).at[spots[1]].set(high)


def block_levels(key, shape, pieces, smallest, top_value):
    gain = 1.0
    for axis_at, parts in pieces:
        draws = jax.random.uniform(jax.random.fold_in(jax.random.fold_in(key, 6), axis_at), (parts,), jnp.float32, smallest / len(pieces), top_value / len(pieces))
        gain = gain * jnp.repeat(jnp.exp(draws), shape[axis_at] // parts).reshape((-1,) + (1,) * (len(shape) - 1 - axis_at))
    return gain


def rank_table(count, lean):
    weights = [(1 << 20) // math.isqrt(grade ** lean) + 1 for grade in range(1, count + 1)]
    deviation = 1 + sum(weights) // (1 << 30)
    return np.cumsum(np.array([max(1, weight // deviation) for weight in weights]))


def ranked(rng, extent, number_of, lean):
    listing = rank_table(number_of, lean)
    lot = jax.random.randint(jax.random.fold_in(rng, 1), extent, 0, int(listing[number_of - 1]))
    rank = jnp.searchsorted(jnp.asarray(listing, jnp.int32), lot, side="right")
    return jax.random.permutation(jax.random.fold_in(rng, 2), number_of)[rank].astype(jnp.int32)


def choose_distinct(stream_key, rows, amount, top, lift):
    sequence = jax.random.permutation(jax.random.fold_in(stream_key, 1), amount)
    pull = sequence
    for power in range(3):
        pull = pull * pull // amount
    pull = pull * lift // amount
    chance = jax.random.randint(jax.random.fold_in(stream_key, 2), (rows, amount), 0, 4096) + pull
    sure = jax.random.permutation(jax.random.fold_in(stream_key, 3), rows)[jnp.arange(amount) % rows]
    chance = jnp.where(jnp.arange(rows)[:, None] == sure[None, :], 1 << 14, chance)
    priority = chance * amount + jnp.arange(amount)
    return lax.top_k(priority.astype(jnp.int32), top)[1].astype(jnp.int32)


def bell_draw(key, extent, scale, most, cuts=(), kind=jnp.bfloat16):
    level = block_levels(key, extent, cuts, -0.22, 0.18) if cuts else 1.0
    result = jax.random.normal(key, extent, jnp.float32) * scale * level
    return jnp.minimum(jnp.maximum(result, -most), most).astype(kind)


def setup_inputs(seed: int = 0) -> dict:
    key_of = jax.random.split(jax.random.key(seed), 10)
    start_state = bell_draw(key_of[0], (PATHS, F), 1.0, 6.0, ((0, 32),), jnp.float32)
    shocks = bell_draw(key_of[1], (STEPS, PATHS, F), 1.0, 6.0, ((1, 32),))
    loading = bell_draw(key_of[2], (F, F), F ** -0.5, 0.125)
    decay = jnp.clip(jax.random.uniform(key_of[3], (F,), jnp.float32, 0.5, 1.0), 0.5, 1.0)
    factor_lists = choose_distinct(key_of[4], SETS, F, K, 512)
    delta = bell_draw(key_of[5], (SETS, K), K ** -0.5, 0.75, ((0, 8),))
    gamma = bell_draw(key_of[6], (SETS, K, K), (K * K) ** -0.5, 0.09375, ((0, 8),))
    currency = place_ends(jax.random.randint(key_of[7], (SETS,), 0, NCUR), jax.random.fold_in(key_of[7], 1), 0, NCUR - 1).astype(jnp.int32)
    owner = place_ends(ranked(key_of[8], (SETS,), CPS, 2), jax.random.fold_in(key_of[8], 3), 0, CPS - 1).astype(jnp.int32)
    return dict(start_state=start_state, shocks=shocks, loading=loading, decay=decay, factor_lists=factor_lists, delta=delta, gamma=gamma, currency=currency, owner=owner)


def value_block(slab, lists_b, delta_b, gamma_b, cur_b):
    rows = slab.shape[0]
    count = lists_b.shape[0]
    picked = jnp.take(slab, lists_b.reshape(-1), axis=1).reshape(rows, count, lists_b.shape[1])
    curved = jnp.einsum('psk,skl->psl', picked.astype(jnp.float32), gamma_b.astype(jnp.float32))
    linear = delta_b.astype(jnp.float32)[None] + 0.5 * curved
    local = jnp.sum(picked.astype(jnp.float32) * linear, axis=2)
    rates = jnp.exp(0.2 * jnp.take(slab, cur_b, axis=1).astype(jnp.float32))
    return (local * rates).T

def revalue(slab, lists, delta, gamma, cur):
    total = lists.shape[0]
    width = math.gcd(16, total)
    blocks = total // width
    depth = lists.shape[1]
    stacked = lax.map(lambda a: value_block(slab, a[0], a[1], a[2], a[3]), (lists.reshape(blocks, width, depth), delta.reshape(blocks, width, depth), gamma.reshape(blocks, width, depth, depth), cur.reshape(blocks, width)))
    return stacked.reshape(total, slab.shape[0])

def regress(gram, moments, total):
    size = gram.shape[0]
    chol = jnp.linalg.cholesky(gram / total + 0.001 * jnp.eye(size, dtype=jnp.float32))
    middle = lax.linalg.triangular_solve(chol, moments / total, left_side=True, lower=True)
    return lax.linalg.triangular_solve(chol, middle, left_side=True, lower=True, transpose_a=True)

def reference(start_state, shocks, loading, decay, factor_lists, delta, gamma, currency, owner):
    high = lax.Precision.HIGHEST
    onehot = (owner[None, :] == jnp.arange(CPS, dtype=jnp.int32)[:, None]).astype(jnp.float32)
    state = start_state
    results = []
    for step in range(STEPS):
        state = decay[None, :] * state + jnp.dot(shocks[step].astype(jnp.float32), loading.astype(jnp.float32), preferred_element_type=jnp.float32)
        slab = state.astype(jnp.bfloat16)
        values = revalue(slab, factor_lists, delta, gamma, currency)
        netted = jnp.dot(onehot, values, precision=high)
        ones = jnp.ones((1, slab.shape[0]), jnp.float32)
        basis = jnp.concatenate([ones, slab[:, :NB].astype(jnp.float32).T], axis=0)
        gram = jnp.dot(basis, basis.T, precision=high)
        moments = jnp.dot(basis, netted.T, precision=high)
        coef = regress(gram, moments, PATHS)
        fitted = jnp.dot(coef.T, basis, precision=high)
        results.append(jnp.maximum(netted - 0.9 * fitted, 0.0))
    return (jnp.stack(results), state)
```

```python
import functools

import jax
import jax.numpy as jnp
from jax import lax
from jax.experimental import pallas as pl
from jax.experimental.pallas import tpu as pltpu
from jax.sharding import PartitionSpec as P

NB = 16
STEPS = 2
CP_DEV = 8
LANES = 128
CHUNK = 512
GROUP = 8
MESH = pl.DeviceIdType.MESH
HIGH = lax.Precision.HIGHEST
CONTRACT_LANES = (((1,), (1,)), ((), ()))


def sweep_inverse(a, size):
    rows = lax.broadcasted_iota(jnp.int32, a.shape, 0)
    cols = lax.broadcasted_iota(jnp.int32, a.shape, 1)
    for k in range(size):
        row = a[k : k + 1, :]
        col = a[:, k : k + 1]
        inv = 1.0 / a[k : k + 1, k : k + 1]
        scaled = row * inv
        update = a - col * scaled
        update = jnp.where(cols == k, col * inv, update)
        update = jnp.where(rows == k, jnp.where(cols == k, -inv, scaled), update)
        a = update
    return -a


def kernel(
    groups, zs, total_paths,
    start_hbm, shocks_hbm, loading_hbm, decay_ref, lists_hbm, delta_ref, gamma_hbm, cur_hbm, owner_ref,
    expo_ref, end_hbm,
    start_v, shocks_v, load_v, lists_s, cur_s, gin_v, end_v,
    gath, slab_t, gam, dlin, rates, xg, vals, basis, parts, rs, gsend, grecv, msend, mrecv,
    load_sem, misc_sem, slab_send, slab_fwd, slab_recv, rs_send, rs_recv, g_send, g_recv, m_send, m_recv,
):
    paths_dev = start_v.shape[0]
    factors = start_v.shape[1]
    depth, sets = lists_s.shape
    group_paths = paths_dev * groups
    pblocks = group_paths // LANES
    cc = STEPS * pblocks
    chunks = factors // CHUNK
    half = depth // 2
    cps = CP_DEV * groups
    width = NB + 1

    me = lax.axis_index("set")
    mz = lax.axis_index("path")
    sibling = me + 1 - 2 * lax.rem(me, 2)

    c_shocks = pltpu.make_async_copy(shocks_hbm, shocks_v, misc_sem.at[0])
    c_start = pltpu.make_async_copy(start_hbm, start_v, misc_sem.at[1])
    c_shocks.start()
    c_start.start()
    c_load = []
    for c in range(chunks):
        cols = pl.ds(c * CHUNK, CHUNK)
        cp = pltpu.make_async_copy(loading_hbm.at[:, cols], load_v.at[:, cols], load_sem.at[c])
        cp.start()
        c_load.append(cp)
    c_gamma = pltpu.make_async_copy(gamma_hbm, gin_v, misc_sem.at[2])
    c_lists = pltpu.make_async_copy(lists_hbm, lists_s, misc_sem.at[3])
    c_cur = pltpu.make_async_copy(cur_hbm, cur_s, misc_sem.at[4])
    c_gamma.start()
    c_lists.start()
    c_cur.start()

    barrier = pltpu.get_barrier_semaphore()
    for i in range(1, groups):
        pl.semaphore_signal(barrier, inc=1, device_id={"set": lax.rem(me + i, groups)}, device_id_type=MESH)
    for i in range(1, zs):
        pl.semaphore_signal(barrier, inc=1, device_id={"path": lax.rem(mz + i, zs)}, device_id_type=MESH)

    def slab_copy(owner, c, send, to):
        spot = gath.at[owner, :, pl.ds(c * CHUNK, CHUNK)]
        return pltpu.make_async_remote_copy(
            src_ref=spot, dst_ref=spot, send_sem=send, recv_sem=slab_recv.at[owner, c],
            device_id={"set": to}, device_id_type=MESH)

    sends = []
    c_shocks.wait()
    c_start.wait()
    for c in range(chunks):
        cols = pl.ds(c * CHUNK, CHUNK)
        c_load[c].wait()
        moved = jnp.dot(shocks_v[...], load_v[:, cols], preferred_element_type=jnp.float32)
        decay = decay_ref[:, cols]
        first = decay * start_v[:, cols] + moved[:paths_dev]
        second = decay * first + moved[paths_dev:]
        end_v[:, cols] = second
        gath[me, :paths_dev, cols] = first.astype(jnp.bfloat16)
        gath[me, paths_dev:, cols] = second.astype(jnp.bfloat16)
        if c == 0:
            pl.semaphore_wait(barrier, groups - 1 + zs - 1)
        for i in range(1, groups // 2):
            cp = slab_copy(me, c, slab_send.at[i, c], lax.rem(me + 2 * i, groups))
            cp.start()
            sends.append(cp)
        cp = slab_copy(me, c, slab_send.at[0, c], sibling)
        cp.start()
        sends.append(cp)
    c_end = pltpu.make_async_copy(end_v, end_hbm, misc_sem.at[5])
    c_end.start()

    c_gamma.wait()

    def relay(m, carry):
        upper = gin_v[pl.ds(pl.multiple_of(m * depth, depth), depth), :]
        lower = gin_v[pl.ds(pl.multiple_of((m + half) * depth, depth), depth), :]
        both = jnp.concatenate([upper, lower], axis=0).astype(jnp.float32)
        gam[pl.ds(m, sets, stride=half), :] = both.T
        return carry

    lax.fori_loop(0, half, relay, 0, unroll=4)
    dlin[...] = delta_ref[...].astype(jnp.float32).T

    def forward(c):
        for i in range(1, groups // 2):
            src = lax.rem(me + 2 * i, groups)
            slab_copy(src, c, slab_fwd.at[i, c], sibling).wait_recv()
            cp = slab_copy(src, c, slab_fwd.at[i, c], sibling)
            cp.start()
            sends.append(cp)

    def turn(c):
        slab_copy(sibling, c, slab_send.at[0, c], sibling).wait_recv()
        for i in range(1, groups // 2):
            slab_copy(lax.rem(sibling + 2 * i, groups), c, slab_fwd.at[i, c], sibling).wait_recv()
        for step in range(STEPS):
            for b in range(CHUNK // LANES):
                f0 = c * CHUNK + b * LANES
                block = gath[:, step * paths_dev : (step + 1) * paths_dev, f0 : f0 + LANES]
                block = block.reshape(group_paths, LANES).astype(jnp.float32).T
                for q in range(pblocks):
                    slab_t[pl.ds(f0 * cc + step * pblocks + q, LANES, stride=cc), :] = block[
                        :, q * LANES : (q + 1) * LANES
                    ]

    for c in range(chunks):
        forward(c)
        if c > 0:
            turn(c - 1)
    turn(chunks - 1)

    rates[...] = jnp.exp(0.2 * slab_t[: NB * cc, :])
    basis[...] = jnp.zeros_like(basis)
    for step in range(STEPS):
        for q in range(pblocks):
            basis[step, :NB, q * LANES : (q + 1) * LANES] = slab_t[pl.ds(step * pblocks + q, NB, stride=cc), :]
        basis[step, NB : NB + 1, :] = jnp.ones((1, group_paths), jnp.float32)
        gsend[step] = lax.dot_general(
            basis[step, : NB + 8, :], basis[step], CONTRACT_LANES, precision=HIGH,
            preferred_element_type=jnp.float32)
    for i in range(1, zs):
        cp = pltpu.make_async_remote_copy(
            src_ref=gsend, dst_ref=grecv.at[i], send_sem=g_send.at[i], recv_sem=g_recv.at[i],
            device_id={"path": lax.rem(mz + i, zs)}, device_id_type=MESH)
        cp.start()
        sends.append(cp)

    c_lists.wait()
    c_cur.wait()

    def revalue(g, carry):
        for u in range(GROUP):
            j = g * GROUP + u
            for k in range(depth):
                at = lists_s[k, j] * cc
                xg[u, k * cc : (k + 1) * cc, :] = slab_t[pl.ds(at, cc), :]
        rows = []
        for u in range(GROUP):
            j = g * GROUP + u
            x = jnp.concatenate([xg[u, pl.ds(c, depth, stride=cc), :] for c in range(cc)], axis=1)
            pair = gam[pl.ds(pl.multiple_of(j * half, half), half), :]
            linear = jnp.broadcast_to(dlin[pl.ds(j, 1), :], (16, depth))
            left = jnp.concatenate([pair[:, :depth], pair[:, depth:], linear], axis=0)
            prod = jnp.dot(left.astype(jnp.bfloat16), x.astype(jnp.bfloat16), preferred_element_type=jnp.float32)
            local = prod[depth : depth + 1] + 0.5 * jnp.sum(x * prod[:depth], axis=0, keepdims=True)
            at = cur_s[j] * cc
            rate = jnp.concatenate([rates[pl.ds(at + c, 1), :] for c in range(cc)], axis=1)
            rows.append(local * rate)
        vals[pl.ds(pl.multiple_of(g * GROUP, GROUP), GROUP), :] = jnp.concatenate(rows, axis=0)
        return carry

    lax.fori_loop(0, sets // GROUP, revalue, 0)

    owns = lax.broadcasted_iota(jnp.int32, (cps, sets), 0) == owner_ref[...]
    summed = jnp.dot(owns.astype(jnp.float32), vals[...], precision=HIGH, preferred_element_type=jnp.float32)
    parts[...] = summed.reshape(groups, CP_DEV, cc * LANES)
    for i in range(1, groups):
        to = lax.rem(me + i, groups)
        cp = pltpu.make_async_remote_copy(
            src_ref=parts.at[to], dst_ref=rs.at[i], send_sem=rs_send.at[i], recv_sem=rs_recv.at[i],
            device_id={"set": to}, device_id_type=MESH)
        cp.start()
        sends.append(cp)

    for i in range(1, zs):
        pltpu.make_async_remote_copy(
            src_ref=gsend, dst_ref=grecv.at[i], send_sem=g_send.at[i], recv_sem=g_recv.at[i],
            device_id={"path": lax.rem(mz + i, zs)}, device_id_type=MESH).wait_recv()
    eye = (lax.broadcasted_iota(jnp.int32, (NB + 8, LANES), 0) == lax.broadcasted_iota(jnp.int32, (NB + 8, LANES), 1))
    ridge = jnp.where(eye & (lax.broadcasted_iota(jnp.int32, (NB + 8, LANES), 0) < width), 0.001, 0.0)
    inverses = []
    for step in range(STEPS):
        gram = gsend[step]
        for i in range(1, zs):
            gram = gram + grecv[i, step]
        inverses.append(sweep_inverse(gram / total_paths + ridge, width))

    netted = parts[me]
    for i in range(1, groups):
        pltpu.make_async_remote_copy(
            src_ref=parts.at[0], dst_ref=rs.at[i], send_sem=rs_send.at[i], recv_sem=rs_recv.at[i],
            device_id={"set": lax.rem(me + i, groups)}, device_id_type=MESH).wait_recv()
        netted = netted + rs[i]
    for step in range(STEPS):
        msend[step] = lax.dot_general(
            netted[:, step * group_paths : (step + 1) * group_paths], basis[step], CONTRACT_LANES, precision=HIGH,
            preferred_element_type=jnp.float32)
    for i in range(1, zs):
        cp = pltpu.make_async_remote_copy(
            src_ref=msend, dst_ref=mrecv.at[i], send_sem=m_send.at[i], recv_sem=m_recv.at[i],
            device_id={"path": lax.rem(mz + i, zs)}, device_id_type=MESH)
        cp.start()
        sends.append(cp)
    for i in range(1, zs):
        pltpu.make_async_remote_copy(
            src_ref=msend, dst_ref=mrecv.at[i], send_sem=m_send.at[i], recv_sem=m_recv.at[i],
            device_id={"path": lax.rem(mz + i, zs)}, device_id_type=MESH).wait_recv()
    for step in range(STEPS):
        moments = msend[step]
        for i in range(1, zs):
            moments = moments + mrecv[i, step]
        moments = moments / total_paths
        coef = jnp.dot(moments[:, : NB + 8], inverses[step], precision=HIGH, preferred_element_type=jnp.float32)
        fitted = jnp.dot(
            coef[:, : NB + 8], basis[step, : NB + 8, :], precision=HIGH, preferred_element_type=jnp.float32)
        mine = netted[:, step * group_paths : (step + 1) * group_paths]
        expo_ref[step] = jnp.maximum(mine - 0.9 * fitted, 0.0)

    for cp in sends:
        cp.wait_send()
    c_end.wait()


def per_device(start_state, shocks, loading, decay, factor_lists, delta, gamma, currency, owner):
    groups = lax.axis_size("set")
    zs = lax.axis_size("path")
    paths_dev, factors = start_state.shape
    sets, depth = factor_lists.shape
    group_paths = paths_dev * groups
    cc = STEPS * group_paths // LANES
    chunks = factors // CHUNK
    any_spec = pl.BlockSpec(memory_space=pl.ANY)
    vmem = pl.BlockSpec(memory_space=pltpu.VMEM)
    f32, bf16 = jnp.float32, jnp.bfloat16
    dma = pltpu.SemaphoreType.DMA
    return pl.pallas_call(
        functools.partial(kernel, groups, zs, paths_dev * groups * zs),
        out_shape=(
            jax.ShapeDtypeStruct((STEPS, CP_DEV, group_paths), f32),
            jax.ShapeDtypeStruct((paths_dev, factors), f32),
        ),
        in_specs=[any_spec, any_spec, any_spec, vmem, any_spec, vmem, any_spec, any_spec, vmem],
        out_specs=(vmem, any_spec),
        scratch_shapes=[
            pltpu.VMEM((paths_dev, factors), f32),
            pltpu.VMEM((STEPS * paths_dev, factors), bf16),
            pltpu.VMEM((factors, factors), bf16),
            pltpu.SMEM((depth, sets), jnp.int32),
            pltpu.SMEM((sets,), jnp.int32),
            pltpu.VMEM((depth * depth, sets), bf16),
            pltpu.VMEM((paths_dev, factors), f32),
            pltpu.VMEM((groups, STEPS * paths_dev, factors), bf16),
            pltpu.VMEM((factors * cc, LANES), f32),
            pltpu.VMEM((sets * depth // 2, 2 * depth), f32),
            pltpu.VMEM((sets, depth), f32),
            pltpu.VMEM((NB * cc, LANES), f32),
            pltpu.VMEM((GROUP, depth * cc, LANES), f32),
            pltpu.VMEM((sets, cc * LANES), f32),
            pltpu.VMEM((STEPS, LANES, group_paths), f32),
            pltpu.VMEM((groups, CP_DEV, cc * LANES), f32),
            pltpu.VMEM((groups, CP_DEV, cc * LANES), f32),
            pltpu.VMEM((STEPS, NB + 8, LANES), f32),
            pltpu.VMEM((zs, STEPS, NB + 8, LANES), f32),
            pltpu.VMEM((STEPS, CP_DEV, LANES), f32),
            pltpu.VMEM((zs, STEPS, CP_DEV, LANES), f32),
            dma((chunks,)),
            dma((6,)),
            dma((groups, chunks)),
            dma((groups, chunks)),
            dma((groups, chunks)),
            dma((groups,)),
            dma((groups,)),
            dma((zs,)),
            dma((zs,)),
            dma((zs,)),
            dma((zs,)),
        ],
        compiler_params=pltpu.CompilerParams(
            collective_id=0, has_side_effects=True, vmem_limit_bytes=48 * 1024 * 1024
        ),
    )(
        start_state,
        shocks.reshape(STEPS * paths_dev, factors),
        loading,
        decay.reshape(1, factors),
        factor_lists.T,
        delta.T,
        jnp.transpose(gamma, (1, 2, 0)).reshape(depth * depth, sets),
        currency,
        owner.reshape(1, sets),
    )


def solution(mesh):
    return jax.shard_map(
        per_device,
        mesh=mesh,
        in_specs=(
            P(("path", "set"), None),
            P(None, ("path", "set"), None),
            P(),
            P(),
            P("set", None),
            P("set", None),
            P("set", None, None),
            P("set"),
            P("set"),
        ),
        out_specs=(P(None, "set", "path"), P(("path", "set"), None)),
        check_vma=False,
    )
```

```python
import functools

import jax
import jax.numpy as jnp
from jax import lax
from jax.experimental import pallas as pl
from jax.experimental.pallas import tpu as pltpu
from jax.sharding import PartitionSpec as P

NB = 16
STEPS = 2
CP_DEV = 8
LANES = 128
CHUNK = 512
PAD = 8
GROUP = 8
MESH = pl.DeviceIdType.MESH
HIGH = lax.Precision.HIGHEST
CONTRACT_LANES = (((1,), (1,)), ((), ()))


def sweep_inverse(a, size):
    rows = lax.broadcasted_iota(jnp.int32, a.shape, 0)
    cols = lax.broadcasted_iota(jnp.int32, a.shape, 1)
    for k in range(size):
        row = a[k : k + 1, :]
        col = a[:, k : k + 1]
        inv = 1.0 / a[k : k + 1, k : k + 1]
        scaled = row * inv
        update = a - col * scaled
        update = jnp.where(cols == k, col * inv, update)
        update = jnp.where(rows == k, jnp.where(cols == k, -inv, scaled), update)
        a = update
    return -a


def kernel(
    groups, zs, total_paths,
    start_hbm, shocks_hbm, loading_hbm, decay_hbm, lists_hbm, delta_hbm, gamma_hbm, cur_hbm, owner_hbm,
    expo_hbm, end_hbm,
    start_v, shocks_v, load_v, decay_ref, lists_s, delta_ref, cur_s, owner_ref, gin_v, end_v, expo_ref,
    gath, slab_t, gam, dlin, left, rates, xg, vals, basis, parts, rs, gsend, grecv, msend, mrecv,
    load_sem, misc_sem, slab_send, slab_fwd, slab_recv, rs_send, rs_recv, g_send, g_recv, m_send, m_recv,
):
    paths_dev = start_v.shape[0]
    factors = start_v.shape[1]
    depth, sets = lists_s.shape
    group_paths = paths_dev * groups
    pblocks = group_paths // LANES
    cc = STEPS * pblocks
    chunks = factors // CHUNK
    half = depth // 2
    cps = CP_DEV * groups
    width = NB + 1

    me = lax.axis_index("set")
    mz = lax.axis_index("path")
    sibling = me + 1 - 2 * lax.rem(me, 2)

    c_shocks = pltpu.make_async_copy(shocks_hbm, shocks_v, misc_sem.at[0])
    c_start = pltpu.make_async_copy(start_hbm, start_v, misc_sem.at[1])
    c_decay = pltpu.make_async_copy(decay_hbm, decay_ref, misc_sem.at[8])
    c_shocks.start()
    c_start.start()
    c_decay.start()
    c_load = []
    for c in range(chunks):
        cols = pl.ds(c * CHUNK, CHUNK)
        cp = pltpu.make_async_copy(loading_hbm.at[:, cols], load_v.at[:, cols], load_sem.at[c])
        cp.start()
        c_load.append(cp)
    c_gamma = pltpu.make_async_copy(gamma_hbm, gin_v, misc_sem.at[2])
    c_lists = pltpu.make_async_copy(lists_hbm, lists_s, misc_sem.at[3])
    c_cur = pltpu.make_async_copy(cur_hbm, cur_s, misc_sem.at[4])
    c_delta = pltpu.make_async_copy(delta_hbm, delta_ref, misc_sem.at[6])
    c_owner = pltpu.make_async_copy(owner_hbm, owner_ref, misc_sem.at[7])
    c_gamma.start()
    c_delta.start()
    c_lists.start()
    c_cur.start()
    c_owner.start()

    barrier = pltpu.get_barrier_semaphore()
    for i in range(1, groups):
        pl.semaphore_signal(barrier, inc=1, device_id={"set": lax.rem(me + i, groups)}, device_id_type=MESH)
    for i in range(1, zs):
        pl.semaphore_signal(barrier, inc=1, device_id={"path": lax.rem(mz + i, zs)}, device_id_type=MESH)

    def slab_copy(owner, c, send, to):
        spot = gath.at[owner, :, pl.ds(c * CHUNK, CHUNK)]
        return pltpu.make_async_remote_copy(
            src_ref=spot, dst_ref=spot, send_sem=send, recv_sem=slab_recv.at[owner, c],
            device_id={"set": to}, device_id_type=MESH)

    sends = []
    c_shocks.wait()
    c_start.wait()
    c_decay.wait()
    for c in range(chunks):
        cols = pl.ds(c * CHUNK, CHUNK)
        c_load[c].wait()
        moved = jnp.dot(shocks_v[...], load_v[:, cols], preferred_element_type=jnp.float32)
        decay = decay_ref[:, cols]
        first = decay * start_v[:, cols] + moved[:paths_dev]
        second = decay * first + moved[paths_dev:]
        end_v[:, cols] = second
        gath[me, :paths_dev, cols] = first.astype(jnp.bfloat16)
        gath[me, paths_dev:, cols] = second.astype(jnp.bfloat16)
        if c == 0:
            pl.semaphore_wait(barrier, groups - 1 + zs - 1)
        for i in range(1, groups // 2):
            cp = slab_copy(me, c, slab_send.at[i, c], lax.rem(me + 2 * i, groups))
            cp.start()
            sends.append(cp)
        cp = slab_copy(me, c, slab_send.at[0, c], sibling)
        cp.start()
        sends.append(cp)
    c_end = pltpu.make_async_copy(end_v, end_hbm, misc_sem.at[5])
    c_end.start()

    c_gamma.wait()

    def relay(m, carry):
        upper = gin_v[pl.ds(pl.multiple_of(m * depth, depth), depth), :]
        lower = gin_v[pl.ds(pl.multiple_of((m + half) * depth, depth), depth), :]
        both = jnp.concatenate([upper, lower], axis=0).astype(jnp.float32)
        gam[pl.ds(m, sets, stride=half), :] = both.T
        return carry

    lax.fori_loop(0, half, relay, 0, unroll=4)
    c_delta.wait()
    dlin[...] = delta_ref[...].astype(jnp.float32).T

    def prepare(j, carry):
        pair = gam[pl.ds(pl.multiple_of(j * half, half), half), :]
        linear = jnp.broadcast_to(dlin[pl.ds(j, 1), :], (16, depth))
        left[j] = jnp.concatenate([pair[:, :depth], pair[:, depth:], linear], axis=0).astype(jnp.bfloat16)
        return carry

    lax.fori_loop(0, sets, prepare, 0, unroll=4)

    def forward(c):
        for i in range(1, groups // 2):
            src = lax.rem(me + 2 * i, groups)
            slab_copy(src, c, slab_fwd.at[i, c], sibling).wait_recv()
            cp = slab_copy(src, c, slab_fwd.at[i, c], sibling)
            cp.start()
            sends.append(cp)

    def turn(c):
        slab_copy(sibling, c, slab_send.at[0, c], sibling).wait_recv()
        for i in range(1, groups // 2):
            slab_copy(lax.rem(sibling + 2 * i, groups), c, slab_fwd.at[i, c], sibling).wait_recv()
        for step in range(STEPS):
            for b in range(CHUNK // LANES):
                f0 = c * CHUNK + b * LANES
                block = gath[:, step * paths_dev : (step + 1) * paths_dev, f0 : f0 + LANES]
                block = block.reshape(group_paths, LANES).astype(jnp.float32).T
                for q in range(pblocks):
                    slab_t[pl.ds(PAD + f0 * cc + step * pblocks + q, LANES, stride=cc), :] = block[
                        :, q * LANES : (q + 1) * LANES
                    ]

    for c in range(chunks):
        forward(c)
        if c > 0:
            turn(c - 1)
    turn(chunks - 1)

    rates[...] = jnp.exp(0.2 * slab_t[PAD : PAD + NB * cc, :])
    basis[...] = jnp.zeros_like(basis)
    for step in range(STEPS):
        for q in range(pblocks):
            basis[step, :NB, q * LANES : (q + 1) * LANES] = slab_t[pl.ds(PAD + step * pblocks + q, NB, stride=cc), :]
        basis[step, NB : NB + 1, :] = jnp.ones((1, group_paths), jnp.float32)
        gsend[step] = lax.dot_general(
            basis[step, : NB + 8, :], basis[step], CONTRACT_LANES, precision=HIGH,
            preferred_element_type=jnp.float32)
    for i in range(1, zs):
        cp = pltpu.make_async_remote_copy(
            src_ref=gsend, dst_ref=grecv.at[i], send_sem=g_send.at[i], recv_sem=g_recv.at[i],
            device_id={"path": lax.rem(mz + i, zs)}, device_id_type=MESH)
        cp.start()
        sends.append(cp)

    c_lists.wait()
    c_cur.wait()

    merged = max(1, PAD // cc)
    span = merged * cc
    sublane = lax.broadcasted_iota(jnp.int32, (span, LANES), 0)

    def revalue(g, carry):
        for u in range(GROUP):
            j = g * GROUP + u
            for k in range(0, depth, merged):
                rows = slab_t[pl.ds(lists_s[k, j] * cc + PAD, span), :]
                for r in range(1, merged):
                    window = slab_t[pl.ds(lists_s[k + r, j] * cc + (PAD - r * cc), span), :]
                    rows = jnp.where(sublane >= r * cc, window, rows)
                xg[u, k * cc : k * cc + span, :] = rows
        rows = []
        for u in range(GROUP):
            j = g * GROUP + u
            x = jnp.concatenate([xg[u, pl.ds(c, depth, stride=cc), :] for c in range(cc)], axis=1)
            prod = jnp.dot(left[j], x.astype(jnp.bfloat16), preferred_element_type=jnp.float32)
            local = prod[depth : depth + 1] + 0.5 * jnp.sum(x * prod[:depth], axis=0, keepdims=True)
            at = cur_s[j] * cc
            rate = jnp.concatenate([rates[pl.ds(at + c, 1), :] for c in range(cc)], axis=1)
            rows.append(local * rate)
        vals[pl.ds(pl.multiple_of(g * GROUP, GROUP), GROUP), :] = jnp.concatenate(rows, axis=0)
        return carry

    lax.fori_loop(0, sets // GROUP, revalue, 0)

    c_owner.wait()
    owns = lax.broadcasted_iota(jnp.int32, (cps, sets), 0) == owner_ref[...]
    summed = jnp.dot(owns.astype(jnp.float32), vals[...], precision=HIGH, preferred_element_type=jnp.float32)
    parts[...] = summed.reshape(groups, CP_DEV, cc * LANES)
    for i in range(1, groups):
        to = lax.rem(me + i, groups)
        cp = pltpu.make_async_remote_copy(
            src_ref=parts.at[to], dst_ref=rs.at[i], send_sem=rs_send.at[i], recv_sem=rs_recv.at[i],
            device_id={"set": to}, device_id_type=MESH)
        cp.start()
        sends.append(cp)

    for i in range(1, zs):
        pltpu.make_async_remote_copy(
            src_ref=gsend, dst_ref=grecv.at[i], send_sem=g_send.at[i], recv_sem=g_recv.at[i],
            device_id={"path": lax.rem(mz + i, zs)}, device_id_type=MESH).wait_recv()
    eye = (lax.broadcasted_iota(jnp.int32, (NB + 8, LANES), 0) == lax.broadcasted_iota(jnp.int32, (NB + 8, LANES), 1))
    ridge = jnp.where(eye & (lax.broadcasted_iota(jnp.int32, (NB + 8, LANES), 0) < width), 0.001, 0.0)
    inverses = []
    for step in range(STEPS):
        gram = gsend[step]
        for i in range(1, zs):
            gram = gram + grecv[i, step]
        inverses.append(sweep_inverse(gram / total_paths + ridge, width))

    netted = parts[me]
    for i in range(1, groups):
        pltpu.make_async_remote_copy(
            src_ref=parts.at[0], dst_ref=rs.at[i], send_sem=rs_send.at[i], recv_sem=rs_recv.at[i],
            device_id={"set": lax.rem(me + i, groups)}, device_id_type=MESH).wait_recv()
        netted = netted + rs[i]
    for step in range(STEPS):
        msend[step] = lax.dot_general(
            netted[:, step * group_paths : (step + 1) * group_paths], basis[step], CONTRACT_LANES, precision=HIGH,
            preferred_element_type=jnp.float32)
    for i in range(1, zs):
        cp = pltpu.make_async_remote_copy(
            src_ref=msend, dst_ref=mrecv.at[i], send_sem=m_send.at[i], recv_sem=m_recv.at[i],
            device_id={"path": lax.rem(mz + i, zs)}, device_id_type=MESH)
        cp.start()
        sends.append(cp)
    for i in range(1, zs):
        pltpu.make_async_remote_copy(
            src_ref=msend, dst_ref=mrecv.at[i], send_sem=m_send.at[i], recv_sem=m_recv.at[i],
            device_id={"path": lax.rem(mz + i, zs)}, device_id_type=MESH).wait_recv()
    for step in range(STEPS):
        moments = msend[step]
        for i in range(1, zs):
            moments = moments + mrecv[i, step]
        moments = moments / total_paths
        coef = jnp.dot(moments[:, : NB + 8], inverses[step], precision=HIGH, preferred_element_type=jnp.float32)
        fitted = jnp.dot(
            coef[:, : NB + 8], basis[step, : NB + 8, :], precision=HIGH, preferred_element_type=jnp.float32)
        mine = netted[:, step * group_paths : (step + 1) * group_paths]
        expo_ref[step] = jnp.maximum(mine - 0.9 * fitted, 0.0)

    c_expo = pltpu.make_async_copy(expo_ref, expo_hbm, misc_sem.at[9])
    c_expo.start()
    for cp in sends:
        cp.wait_send()
    c_expo.wait()
    c_end.wait()


def per_device(start_state, shocks, loading, decay, factor_lists, delta, gamma, currency, owner):
    groups = lax.axis_size("set")
    zs = lax.axis_size("path")
    paths_dev, factors = start_state.shape
    sets, depth = factor_lists.shape
    group_paths = paths_dev * groups
    cc = STEPS * group_paths // LANES
    chunks = factors // CHUNK
    hbm = pl.BlockSpec(memory_space=pltpu.HBM)
    f32, bf16 = jnp.float32, jnp.bfloat16
    dma = pltpu.SemaphoreType.DMA
    return pl.pallas_call(
        functools.partial(kernel, groups, zs, paths_dev * groups * zs),
        out_shape=(
            jax.ShapeDtypeStruct((STEPS, CP_DEV, group_paths), f32),
            jax.ShapeDtypeStruct((paths_dev, factors), f32),
        ),
        in_specs=[hbm] * 9,
        out_specs=(hbm, hbm),
        scratch_shapes=[
            pltpu.VMEM((paths_dev, factors), f32),
            pltpu.VMEM((STEPS * paths_dev, factors), bf16),
            pltpu.VMEM((factors, factors), bf16),
            pltpu.VMEM((1, factors), f32),
            pltpu.SMEM((depth, sets), jnp.int32),
            pltpu.VMEM((depth, sets), bf16),
            pltpu.SMEM((sets,), jnp.int32),
            pltpu.VMEM((1, sets), jnp.int32),
            pltpu.VMEM((depth * depth, sets), bf16),
            pltpu.VMEM((paths_dev, factors), f32),
            pltpu.VMEM((STEPS, CP_DEV, group_paths), f32),
            pltpu.VMEM((groups, STEPS * paths_dev, factors), bf16),
            pltpu.VMEM((factors * cc + 2 * PAD, LANES), f32),
            pltpu.VMEM((sets * depth // 2, 2 * depth), f32),
            pltpu.VMEM((sets, depth), f32),
            pltpu.VMEM((sets, depth + 16, depth), bf16),
            pltpu.VMEM((NB * cc, LANES), f32),
            pltpu.VMEM((GROUP, depth * cc, LANES), f32),
            pltpu.VMEM((sets, cc * LANES), f32),
            pltpu.VMEM((STEPS, LANES, group_paths), f32),
            pltpu.VMEM((groups, CP_DEV, cc * LANES), f32),
            pltpu.VMEM((groups, CP_DEV, cc * LANES), f32),
            pltpu.VMEM((STEPS, NB + 8, LANES), f32),
            pltpu.VMEM((zs, STEPS, NB + 8, LANES), f32),
            pltpu.VMEM((STEPS, CP_DEV, LANES), f32),
            pltpu.VMEM((zs, STEPS, CP_DEV, LANES), f32),
            dma((chunks,)),
            dma((10,)),
            dma((groups, chunks)),
            dma((groups, chunks)),
            dma((groups, chunks)),
            dma((groups,)),
            dma((groups,)),
            dma((zs,)),
            dma((zs,)),
            dma((zs,)),
            dma((zs,)),
        ],
        compiler_params=pltpu.CompilerParams(
            collective_id=0, has_side_effects=True, vmem_limit_bytes=56 * 1024 * 1024
        ),
    )(
        start_state,
        shocks.reshape(STEPS * paths_dev, factors),
        loading,
        decay.reshape(1, factors),
        factor_lists.T,
        delta.T,
        jnp.transpose(gamma, (1, 2, 0)).reshape(depth * depth, sets),
        currency,
        owner.reshape(1, sets),
    )


def solution(mesh):
    return jax.shard_map(
        per_device,
        mesh=mesh,
        in_specs=(
            P(("path", "set"), None),
            P(None, ("path", "set"), None),
            P(),
            P(),
            P("set", None),
            P("set", None),
            P("set", None, None),
            P("set"),
            P("set"),
        ),
        out_specs=(P(None, "set", "path"), P(("path", "set"), None)),
        check_vma=False,
    )
```

```python
import functools

import jax
import jax.numpy as jnp
from jax import lax
from jax.experimental import pallas as pl
from jax.experimental.pallas import tpu as pltpu
from jax.sharding import PartitionSpec as P

NB = 16
STEPS = 2
CP_DEV = 8
LANES = 128
CHUNK = 512
PAD = 8
GROUP = 8
MESH = pl.DeviceIdType.MESH
HIGH = lax.Precision.HIGHEST
CONTRACT_LANES = (((1,), (1,)), ((), ()))


def sweep_inverse(a, size):
    rows = lax.broadcasted_iota(jnp.int32, a.shape, 0)
    cols = lax.broadcasted_iota(jnp.int32, a.shape, 1)
    for k in range(size):
        row = a[k : k + 1, :]
        col = a[:, k : k + 1]
        inv = 1.0 / a[k : k + 1, k : k + 1]
        scaled = row * inv
        update = a - col * scaled
        update = jnp.where(cols == k, col * inv, update)
        update = jnp.where(rows == k, jnp.where(cols == k, -inv, scaled), update)
        a = update
    return -a


def kernel(
    groups, zs, total_paths,
    start_hbm, shocks_hbm, loading_hbm, decay_hbm, lists_hbm, delta_hbm, gamma_hbm, cur_hbm, owner_hbm,
    expo_ref, end_v,
    start_v, shocks_v, load_v, decay_ref, lists_s, delta_ref, cur_s, owner_ref, gin_v,
    gath, slab_t, gam, dlin, left, rates, xg, vals, basis, parts, rs, gsend, grecv, msend, mrecv,
    load_sem, misc_sem, slab_send, slab_fwd, slab_recv, rs_send, rs_recv, g_send, g_recv, m_send, m_recv,
):
    paths_dev = start_v.shape[0]
    factors = start_v.shape[1]
    depth, sets = lists_s.shape
    group_paths = paths_dev * groups
    pblocks = group_paths // LANES
    cc = STEPS * pblocks
    chunks = factors // CHUNK
    half = depth // 2
    cps = CP_DEV * groups
    width = NB + 1

    me = lax.axis_index("set")
    mz = lax.axis_index("path")
    sibling = me + 1 - 2 * lax.rem(me, 2)

    c_shocks = pltpu.make_async_copy(shocks_hbm, shocks_v, misc_sem.at[0])
    c_start = pltpu.make_async_copy(start_hbm, start_v, misc_sem.at[1])
    c_decay = pltpu.make_async_copy(decay_hbm, decay_ref, misc_sem.at[8])
    c_shocks.start()
    c_start.start()
    c_decay.start()
    c_load = []
    for c in range(chunks):
        cols = pl.ds(c * CHUNK, CHUNK)
        cp = pltpu.make_async_copy(loading_hbm.at[:, cols], load_v.at[:, cols], load_sem.at[c])
        cp.start()
        c_load.append(cp)
    c_gamma = pltpu.make_async_copy(gamma_hbm, gin_v, misc_sem.at[2])
    c_lists = pltpu.make_async_copy(lists_hbm, lists_s, misc_sem.at[3])
    c_cur = pltpu.make_async_copy(cur_hbm, cur_s, misc_sem.at[4])
    c_delta = pltpu.make_async_copy(delta_hbm, delta_ref, misc_sem.at[6])
    c_owner = pltpu.make_async_copy(owner_hbm, owner_ref, misc_sem.at[7])
    c_gamma.start()
    c_delta.start()
    c_lists.start()
    c_cur.start()
    c_owner.start()

    barrier = pltpu.get_barrier_semaphore()
    for i in range(1, groups):
        pl.semaphore_signal(barrier, inc=1, device_id={"set": lax.rem(me + i, groups)}, device_id_type=MESH)
    for i in range(1, zs):
        pl.semaphore_signal(barrier, inc=1, device_id={"path": lax.rem(mz + i, zs)}, device_id_type=MESH)

    def slab_copy(owner, c, send, to):
        spot = gath.at[owner, :, pl.ds(c * CHUNK, CHUNK)]
        return pltpu.make_async_remote_copy(
            src_ref=spot, dst_ref=spot, send_sem=send, recv_sem=slab_recv.at[owner, c],
            device_id={"set": to}, device_id_type=MESH)

    sends = []
    c_shocks.wait()
    c_start.wait()
    c_decay.wait()
    for c in range(chunks):
        cols = pl.ds(c * CHUNK, CHUNK)
        c_load[c].wait()
        moved = jnp.dot(shocks_v[...], load_v[:, cols], preferred_element_type=jnp.float32)
        decay = decay_ref[:, cols]
        first = decay * start_v[:, cols] + moved[:paths_dev]
        second = decay * first + moved[paths_dev:]
        end_v[:, cols] = second
        gath[me, :paths_dev, cols] = first.astype(jnp.bfloat16)
        gath[me, paths_dev:, cols] = second.astype(jnp.bfloat16)
        if c == 0:
            pl.semaphore_wait(barrier, groups - 1 + zs - 1)
        for i in range(1, groups // 2):
            cp = slab_copy(me, c, slab_send.at[i, c], lax.rem(me + 2 * i, groups))
            cp.start()
            sends.append(cp)
        cp = slab_copy(me, c, slab_send.at[0, c], sibling)
        cp.start()
        sends.append(cp)

    def relay(m, carry):
        upper = gin_v[pl.ds(pl.multiple_of(m * depth, depth), depth), :]
        lower = gin_v[pl.ds(pl.multiple_of((m + half) * depth, depth), depth), :]
        both = jnp.concatenate([upper, lower], axis=0).astype(jnp.float32)
        gam[pl.ds(m, sets, stride=half), :] = both.T
        return carry

    def prepare(j, carry):
        pair = gam[pl.ds(pl.multiple_of(j * half, half), half), :]
        linear = jnp.broadcast_to(dlin[pl.ds(j, 1), :], (16, depth))
        left[j] = jnp.concatenate([pair[:, :depth], pair[:, depth:], linear], axis=0).astype(jnp.bfloat16)
        return carry

    def piece(c):
        early = chunks // 2
        if c == 0:
            c_gamma.wait()
            c_delta.wait()
            dlin[...] = delta_ref[...].astype(jnp.float32).T
        if c < early:
            lax.fori_loop(half * c // early, half * (c + 1) // early, relay, 0, unroll=4)
        else:
            at, late = c - early, chunks - early
            lax.fori_loop(sets * at // late, sets * (at + 1) // late, prepare, 0, unroll=8)

    def forward(c):
        for i in range(1, groups // 2):
            src = lax.rem(me + 2 * i, groups)
            slab_copy(src, c, slab_fwd.at[i, c], sibling).wait_recv()
            cp = slab_copy(src, c, slab_fwd.at[i, c], sibling)
            cp.start()
            sends.append(cp)

    def turn(c):
        slab_copy(sibling, c, slab_send.at[0, c], sibling).wait_recv()
        for i in range(1, groups // 2):
            slab_copy(lax.rem(sibling + 2 * i, groups), c, slab_fwd.at[i, c], sibling).wait_recv()
        for step in range(STEPS):
            for b in range(CHUNK // LANES):
                f0 = c * CHUNK + b * LANES
                block = gath[:, step * paths_dev : (step + 1) * paths_dev, f0 : f0 + LANES]
                block = block.reshape(group_paths, LANES).astype(jnp.float32).T
                for q in range(pblocks):
                    slab_t[pl.ds(PAD + f0 * cc + step * pblocks + q, LANES, stride=cc), :] = block[
                        :, q * LANES : (q + 1) * LANES
                    ]

    def send_gram():
        rates[...] = jnp.exp(0.2 * slab_t[PAD : PAD + NB * cc, :])
        basis[...] = jnp.zeros_like(basis)
        for step in range(STEPS):
            for q in range(pblocks):
                basis[step, :NB, q * LANES : (q + 1) * LANES] = slab_t[
                    pl.ds(PAD + step * pblocks + q, NB, stride=cc), :
                ]
            basis[step, NB : NB + 1, :] = jnp.ones((1, group_paths), jnp.float32)
            gsend[step] = lax.dot_general(
                basis[step, : NB + 8, :], basis[step], CONTRACT_LANES, precision=HIGH,
                preferred_element_type=jnp.float32)
        for i in range(1, zs):
            cp = pltpu.make_async_remote_copy(
                src_ref=gsend, dst_ref=grecv.at[i], send_sem=g_send.at[i], recv_sem=g_recv.at[i],
                device_id={"path": lax.rem(mz + i, zs)}, device_id_type=MESH)
            cp.start()
            sends.append(cp)

    for c in range(chunks):
        piece(c)
        forward(c)
        if c > 0:
            turn(c - 1)
        if c == 1:
            send_gram()
    turn(chunks - 1)

    c_lists.wait()
    c_cur.wait()

    merged = max(1, PAD // cc)
    span = merged * cc
    sublane = lax.broadcasted_iota(jnp.int32, (span, LANES), 0)

    def gather(buf, u, j):
        for k in range(0, depth, merged):
            rows = slab_t[pl.ds(lists_s[k, j] * cc + PAD, span), :]
            for r in range(1, merged):
                window = slab_t[pl.ds(lists_s[k + r, j] * cc + (PAD - r * cc), span), :]
                rows = jnp.where(sublane >= r * cc, window, rows)
            xg[buf, u, k * cc : k * cc + span, :] = rows

    def value(buf, u, j):
        x = jnp.concatenate([xg[buf, u, pl.ds(c, depth, stride=cc), :] for c in range(cc)], axis=1)
        prod = jnp.dot(left[j], x.astype(jnp.bfloat16), preferred_element_type=jnp.float32)
        local = prod[depth : depth + 1] + 0.5 * jnp.sum(x * prod[:depth], axis=0, keepdims=True)
        at = cur_s[j] * cc
        return local * jnp.concatenate([rates[pl.ds(at + c, 1), :] for c in range(cc)], axis=1)

    rounds = sets // GROUP

    def revalue(i, carry):
        for buf in range(2):
            g = 2 * i + buf
            later = lax.rem(g + 1, rounds)
            rows = []
            for u in range(GROUP):
                gather(1 - buf, u, later * GROUP + u)
                rows.append(value(buf, u, g * GROUP + u))
            vals[pl.ds(pl.multiple_of(g * GROUP, GROUP), GROUP), :] = jnp.concatenate(rows, axis=0)
        return carry

    for u in range(GROUP):
        gather(0, u, u)
    lax.fori_loop(0, rounds // 2, revalue, 0)

    c_owner.wait()
    owns = lax.broadcasted_iota(jnp.int32, (cps, sets), 0) == owner_ref[...]
    owns = owns.astype(jnp.bfloat16)
    value_f32 = vals[...]
    high = value_f32.astype(jnp.bfloat16)
    rest = value_f32 - high.astype(jnp.float32)
    middle = rest.astype(jnp.bfloat16)
    low = (rest - middle.astype(jnp.float32)).astype(jnp.bfloat16)
    summed = jnp.dot(
        jnp.concatenate([owns] * 3, axis=1), jnp.concatenate([high, middle, low], axis=0),
        preferred_element_type=jnp.float32)
    parts[...] = summed.reshape(groups, CP_DEV, cc * LANES)
    for i in range(1, groups):
        to = lax.rem(me + i, groups)
        cp = pltpu.make_async_remote_copy(
            src_ref=parts.at[to], dst_ref=rs.at[i], send_sem=rs_send.at[i], recv_sem=rs_recv.at[i],
            device_id={"set": to}, device_id_type=MESH)
        cp.start()
        sends.append(cp)

    for i in range(1, zs):
        pltpu.make_async_remote_copy(
            src_ref=gsend, dst_ref=grecv.at[i], send_sem=g_send.at[i], recv_sem=g_recv.at[i],
            device_id={"path": lax.rem(mz + i, zs)}, device_id_type=MESH).wait_recv()
    eye = (lax.broadcasted_iota(jnp.int32, (NB + 8, LANES), 0) == lax.broadcasted_iota(jnp.int32, (NB + 8, LANES), 1))
    ridge = jnp.where(eye & (lax.broadcasted_iota(jnp.int32, (NB + 8, LANES), 0) < width), 0.001, 0.0)
    fits = []
    for step in range(STEPS):
        gram = gsend[step]
        for i in range(1, zs):
            gram = gram + grecv[i, step]
        inverse = sweep_inverse(gram / total_paths + ridge, width)
        fits.append(jnp.dot(
            inverse[:, : NB + 8], basis[step, : NB + 8, :], precision=HIGH,
            preferred_element_type=jnp.float32) / total_paths)

    netted = parts[me]
    for i in range(1, groups):
        pltpu.make_async_remote_copy(
            src_ref=parts.at[0], dst_ref=rs.at[i], send_sem=rs_send.at[i], recv_sem=rs_recv.at[i],
            device_id={"set": lax.rem(me + i, groups)}, device_id_type=MESH).wait_recv()
        netted = netted + rs[i]
    for step in range(STEPS):
        msend[step] = lax.dot_general(
            netted[:, step * group_paths : (step + 1) * group_paths], basis[step], CONTRACT_LANES, precision=HIGH,
            preferred_element_type=jnp.float32)
    for i in range(1, zs):
        cp = pltpu.make_async_remote_copy(
            src_ref=msend, dst_ref=mrecv.at[i], send_sem=m_send.at[i], recv_sem=m_recv.at[i],
            device_id={"path": lax.rem(mz + i, zs)}, device_id_type=MESH)
        cp.start()
        sends.append(cp)
    for i in range(1, zs):
        pltpu.make_async_remote_copy(
            src_ref=msend, dst_ref=mrecv.at[i], send_sem=m_send.at[i], recv_sem=m_recv.at[i],
            device_id={"path": lax.rem(mz + i, zs)}, device_id_type=MESH).wait_recv()
    for step in range(STEPS):
        moments = msend[step]
        for i in range(1, zs):
            moments = moments + mrecv[i, step]
        fitted = jnp.dot(moments[:, : NB + 8], fits[step], precision=HIGH, preferred_element_type=jnp.float32)
        mine = netted[:, step * group_paths : (step + 1) * group_paths]
        expo_ref[step] = jnp.maximum(mine - 0.9 * fitted, 0.0)

    for cp in sends:
        cp.wait_send()


def per_device(start_state, shocks, loading, decay, factor_lists, delta, gamma, currency, owner):
    groups = lax.axis_size("set")
    zs = lax.axis_size("path")
    paths_dev, factors = start_state.shape
    sets, depth = factor_lists.shape
    group_paths = paths_dev * groups
    cc = STEPS * group_paths // LANES
    chunks = factors // CHUNK
    hbm = pl.BlockSpec(memory_space=pltpu.HBM)
    vmem = pl.BlockSpec(memory_space=pltpu.VMEM)
    f32, bf16 = jnp.float32, jnp.bfloat16
    dma = pltpu.SemaphoreType.DMA
    return pl.pallas_call(
        functools.partial(kernel, groups, zs, paths_dev * groups * zs),
        out_shape=(
            jax.ShapeDtypeStruct((STEPS, CP_DEV, group_paths), f32),
            jax.ShapeDtypeStruct((paths_dev, factors), f32),
        ),
        in_specs=[hbm] * 9,
        out_specs=(vmem, vmem),
        scratch_shapes=[
            pltpu.VMEM((paths_dev, factors), f32),
            pltpu.VMEM((STEPS * paths_dev, factors), bf16),
            pltpu.VMEM((factors, factors), bf16),
            pltpu.VMEM((1, factors), f32),
            pltpu.SMEM((depth, sets), jnp.int32),
            pltpu.VMEM((depth, sets), bf16),
            pltpu.SMEM((sets,), jnp.int32),
            pltpu.VMEM((1, sets), jnp.int32),
            pltpu.VMEM((depth * depth, sets), bf16),
            pltpu.VMEM((groups, STEPS * paths_dev, factors), bf16),
            pltpu.VMEM((factors * cc + 2 * PAD, LANES), f32),
            pltpu.VMEM((sets * depth // 2, 2 * depth), f32),
            pltpu.VMEM((sets, depth), f32),
            pltpu.VMEM((sets, depth + 16, depth), bf16),
            pltpu.VMEM((NB * cc, LANES), f32),
            pltpu.VMEM((2, GROUP, depth * cc, LANES), f32),
            pltpu.VMEM((sets, cc * LANES), f32),
            pltpu.VMEM((STEPS, LANES, group_paths), f32),
            pltpu.VMEM((groups, CP_DEV, cc * LANES), f32),
            pltpu.VMEM((groups, CP_DEV, cc * LANES), f32),
            pltpu.VMEM((STEPS, NB + 8, LANES), f32),
            pltpu.VMEM((zs, STEPS, NB + 8, LANES), f32),
            pltpu.VMEM((STEPS, CP_DEV, LANES), f32),
            pltpu.VMEM((zs, STEPS, CP_DEV, LANES), f32),
            dma((chunks,)),
            dma((10,)),
            dma((groups, chunks)),
            dma((groups, chunks)),
            dma((groups, chunks)),
            dma((groups,)),
            dma((groups,)),
            dma((zs,)),
            dma((zs,)),
            dma((zs,)),
            dma((zs,)),
        ],
        compiler_params=pltpu.CompilerParams(
            collective_id=0, has_side_effects=True, vmem_limit_bytes=40 * 1024 * 1024
        ),
    )(
        start_state,
        shocks.reshape(STEPS * paths_dev, factors),
        loading,
        decay.reshape(1, factors),
        factor_lists.T,
        delta.T,
        jnp.transpose(gamma, (1, 2, 0)).reshape(depth * depth, sets),
        currency,
        owner.reshape(1, sets),
    )


def solution(mesh):
    return jax.shard_map(
        per_device,
        mesh=mesh,
        in_specs=(
            P(("path", "set"), None),
            P(None, ("path", "set"), None),
            P(),
            P(),
            P("set", None),
            P("set", None),
            P("set", None, None),
            P("set"),
            P("set"),
        ),
        out_specs=(P(None, "set", "path"), P(("path", "set"), None)),
        check_vma=False,
    )
```

```python
import functools

import jax
import jax.numpy as jnp
from jax import lax
from jax.experimental import pallas as pl
from jax.experimental.pallas import tpu as pltpu
from jax.sharding import PartitionSpec as P

NB = 16
STEPS = 2
CP_DEV = 8
LANES = 128
CHUNK = 512
PAD = 8
GROUP = 4
MESH = pl.DeviceIdType.MESH
HIGH = lax.Precision.HIGHEST
CONTRACT_LANES = (((1,), (1,)), ((), ()))


def sweep_inverse(a, size):
    rows = lax.broadcasted_iota(jnp.int32, a.shape, 0)
    cols = lax.broadcasted_iota(jnp.int32, a.shape, 1)
    for k in range(size):
        row = a[k : k + 1, :]
        col = a[:, k : k + 1]
        inv = 1.0 / a[k : k + 1, k : k + 1]
        scaled = row * inv
        update = a - col * scaled
        update = jnp.where(cols == k, col * inv, update)
        update = jnp.where(rows == k, jnp.where(cols == k, -inv, scaled), update)
        a = update
    return -a


def kernel(
    groups, zs, total_paths,
    start_hbm, shocks_hbm, loading_hbm, decay_hbm, lists_hbm, delta_hbm, gamma_hbm, cur_hbm, owner_hbm,
    expo_hbm, end_hbm,
    start_v, shocks_v, load_v, decay_ref, lists_s, delta_ref, cur_s, owner_ref, gin_v, end_v, expo_ref,
    gath, slab_t, gam, dlin, left, rates, xg, vals, basis, parts, rs, gsend, grecv, msend, mrecv,
    load_sem, misc_sem, slab_send, slab_fwd, slab_recv, rs_send, rs_recv, g_send, g_recv, m_send, m_recv,
):
    paths_dev = start_v.shape[0]
    factors = start_v.shape[1]
    depth, sets = lists_s.shape
    group_paths = paths_dev * groups
    pblocks = group_paths // LANES
    cc = STEPS * pblocks
    chunks = factors // CHUNK
    half = depth // 2
    rounds = sets // GROUP
    cps = CP_DEV * groups
    width = NB + 1

    me = lax.axis_index("set")
    mz = lax.axis_index("path")
    sibling = me + 1 - 2 * lax.rem(me, 2)

    c_shocks = pltpu.make_async_copy(shocks_hbm, shocks_v, misc_sem.at[0])
    c_start = pltpu.make_async_copy(start_hbm, start_v, misc_sem.at[1])
    c_decay = pltpu.make_async_copy(decay_hbm, decay_ref, misc_sem.at[8])
    c_shocks.start()
    c_start.start()
    c_decay.start()

    def load_copy(c):
        cols = pl.ds(pl.multiple_of(c * CHUNK, CHUNK), CHUNK)
        return pltpu.make_async_copy(loading_hbm.at[:, cols], load_v.at[:, cols], load_sem.at[c])

    for c in range(chunks):
        load_copy(c).start()
    c_gamma = pltpu.make_async_copy(gamma_hbm, gin_v, misc_sem.at[2])
    c_lists = pltpu.make_async_copy(lists_hbm, lists_s, misc_sem.at[3])
    c_cur = pltpu.make_async_copy(cur_hbm, cur_s, misc_sem.at[4])
    c_delta = pltpu.make_async_copy(delta_hbm, delta_ref, misc_sem.at[6])
    c_owner = pltpu.make_async_copy(owner_hbm, owner_ref, misc_sem.at[7])
    c_gamma.start()
    c_delta.start()
    c_lists.start()
    c_cur.start()
    c_owner.start()

    barrier = pltpu.get_barrier_semaphore()
    for i in range(1, groups):
        pl.semaphore_signal(barrier, inc=1, device_id={"set": lax.rem(me + i, groups)}, device_id_type=MESH)
    for i in range(1, zs):
        pl.semaphore_signal(barrier, inc=1, device_id={"path": lax.rem(mz + i, zs)}, device_id_type=MESH)

    def slab_copy(owner, c, send, to):
        spot = gath.at[owner, :, pl.ds(pl.multiple_of(c * CHUNK, CHUNK), CHUNK)]
        return pltpu.make_async_remote_copy(
            src_ref=spot, dst_ref=spot, send_sem=send, recv_sem=slab_recv.at[owner, c],
            device_id={"set": to}, device_id_type=MESH)

    left[...] = jnp.zeros_like(left)

    sends = []
    c_shocks.wait()
    c_start.wait()
    c_decay.wait()
    pl.semaphore_wait(barrier, groups - 1 + zs - 1)

    def evolve(c, carry):
        cols = pl.ds(pl.multiple_of(c * CHUNK, CHUNK), CHUNK)
        load_copy(c).wait()
        moved = jnp.dot(shocks_v[...], load_v[:, cols], preferred_element_type=jnp.float32)
        decay = decay_ref[:, cols]
        first = decay * start_v[:, cols] + moved[:paths_dev]
        second = decay * first + moved[paths_dev:]
        end_v[:, cols] = second
        gath[me, :paths_dev, cols] = first.astype(jnp.bfloat16)
        gath[me, paths_dev:, cols] = second.astype(jnp.bfloat16)
        for i in range(1, groups // 2):
            slab_copy(me, c, slab_send.at[i, c], lax.rem(me + 2 * i, groups)).start()
        slab_copy(me, c, slab_send.at[0, c], sibling).start()
        return carry

    lax.fori_loop(0, chunks, evolve, 0)
    c_end = pltpu.make_async_copy(end_v, end_hbm, misc_sem.at[5])
    c_end.start()

    def relay(m, carry):
        upper = gin_v[pl.ds(pl.multiple_of(m * depth, depth), depth), :]
        lower = gin_v[pl.ds(pl.multiple_of((m + half) * depth, depth), depth), :]
        both = jnp.concatenate([upper, lower], axis=0).astype(jnp.float32)
        gam[pl.ds(m, sets, stride=half), :] = both.T
        return carry

    def prepare(q, carry):
        for u in range(GROUP):
            pair = gam[pl.ds(pl.multiple_of((q * GROUP + u) * half, half), half), :]
            block = jnp.concatenate([pair[:, :depth], pair[:, depth:]], axis=0).astype(jnp.bfloat16)
            left[q, u * depth : (u + 1) * depth, u * depth : (u + 1) * depth] = block
        lines = []
        for u in range(GROUP):
            line = dlin[pl.ds(q * GROUP + u, 1), :]
            none = jnp.zeros_like(line)
            lines.append(jnp.concatenate([none] * u + [line] + [none] * (GROUP - 1 - u), axis=1))
        lines.append(jnp.zeros((16 - GROUP, GROUP * depth), jnp.float32))
        left[q, GROUP * depth :, :] = jnp.concatenate(lines, axis=0).astype(jnp.bfloat16)
        return carry

    def piece(c):
        early = chunks // 2
        if c == 0:
            c_gamma.wait()
            c_delta.wait()
            dlin[...] = delta_ref[...].astype(jnp.float32).T
        if c < early:
            lax.fori_loop(half * c // early, half * (c + 1) // early, relay, 0, unroll=4)
        else:
            at, late = c - early, chunks - early
            lax.fori_loop(rounds * at // late, rounds * (at + 1) // late, prepare, 0, unroll=2)

    def forward(c):
        for i in range(1, groups // 2):
            src = lax.rem(me + 2 * i, groups)
            slab_copy(src, c, slab_fwd.at[i, c], sibling).wait_recv()
            slab_copy(src, c, slab_fwd.at[i, c], sibling).start()

    def turn(c):
        slab_copy(sibling, c, slab_send.at[0, c], sibling).wait_recv()
        for i in range(1, groups // 2):
            slab_copy(lax.rem(sibling + 2 * i, groups), c, slab_fwd.at[i, c], sibling).wait_recv()

        def flip(b, carry):
            f0 = pl.multiple_of(c * CHUNK + b * LANES, LANES)
            for step in range(STEPS):
                block = gath[:, step * paths_dev : (step + 1) * paths_dev, pl.ds(f0, LANES)]
                block = block.reshape(group_paths, LANES).astype(jnp.float32).T
                for q in range(pblocks):
                    slab_t[pl.ds(PAD + f0 * cc + step * pblocks + q, LANES, stride=cc), :] = block[
                        :, q * LANES : (q + 1) * LANES
                    ]
            return carry

        lax.fori_loop(0, CHUNK // LANES, flip, 0, unroll=2)

    def send_gram():
        rates[...] = jnp.exp(0.2 * slab_t[PAD : PAD + NB * cc, :])
        basis[...] = jnp.zeros_like(basis)
        for step in range(STEPS):
            for q in range(pblocks):
                basis[step, :NB, q * LANES : (q + 1) * LANES] = slab_t[
                    pl.ds(PAD + step * pblocks + q, NB, stride=cc), :
                ]
            basis[step, NB : NB + 1, :] = jnp.ones((1, group_paths), jnp.float32)
            gsend[step] = lax.dot_general(
                basis[step, : NB + 8, :], basis[step], CONTRACT_LANES, precision=HIGH,
                preferred_element_type=jnp.float32)
        for i in range(1, zs):
            cp = pltpu.make_async_remote_copy(
                src_ref=gsend, dst_ref=grecv.at[i], send_sem=g_send.at[i], recv_sem=g_recv.at[i],
                device_id={"path": lax.rem(mz + i, zs)}, device_id_type=MESH)
            cp.start()
            sends.append(cp)

    for c in range(chunks):
        piece(c)
        forward(c)
        if c > 0:
            turn(c - 1)
        if c == 1:
            send_gram()
    turn(chunks - 1)

    c_lists.wait()
    c_cur.wait()

    merged = max(1, PAD // cc)
    span = merged * cc
    sublane = lax.broadcasted_iota(jnp.int32, (span, LANES), 0)

    def gather(buf, u, j):
        for k in range(0, depth, merged):
            rows = slab_t[pl.ds(lists_s[k, j] * cc + PAD, span), :]
            for r in range(1, merged):
                window = slab_t[pl.ds(lists_s[k + r, j] * cc + (PAD - r * cc), span), :]
                rows = jnp.where(sublane >= r * cc, window, rows)
            xg[buf, u, k * cc : k * cc + span, :] = rows

    def values(buf, g):
        x = jnp.concatenate(
            [
                jnp.concatenate([xg[buf, u, pl.ds(c, depth, stride=cc), :] for c in range(cc)], axis=1)
                for u in range(GROUP)
            ],
            axis=0,
        )
        prod = jnp.dot(left[g], x.astype(jnp.bfloat16), preferred_element_type=jnp.float32)
        rows = []
        for u in range(GROUP):
            part = slice(u * depth, (u + 1) * depth)
            linear = prod[GROUP * depth + u : GROUP * depth + u + 1]
            local = linear + 0.5 * jnp.sum(x[part] * prod[part], axis=0, keepdims=True)
            at = cur_s[g * GROUP + u] * cc
            rows.append(local * jnp.concatenate([rates[pl.ds(at + c, 1), :] for c in range(cc)], axis=1))
        return rows

    def revalue(i, carry):
        rows = []
        for buf in range(2):
            later = lax.rem(2 * i + buf + 1, rounds)
            for u in range(GROUP):
                gather(1 - buf, u, later * GROUP + u)
            rows += values(buf, 2 * i + buf)
        both = 2 * GROUP
        vals[pl.ds(pl.multiple_of(i * both, both), both), :] = jnp.concatenate(rows, axis=0)
        return carry

    for u in range(GROUP):
        gather(0, u, u)
    lax.fori_loop(0, rounds // 2, revalue, 0)

    c_owner.wait()
    owns = lax.broadcasted_iota(jnp.int32, (cps, sets), 0) == owner_ref[...]
    owns = owns.astype(jnp.bfloat16)
    value_f32 = vals[...]
    high = value_f32.astype(jnp.bfloat16)
    rest = value_f32 - high.astype(jnp.float32)
    middle = rest.astype(jnp.bfloat16)
    low = (rest - middle.astype(jnp.float32)).astype(jnp.bfloat16)
    summed = jnp.dot(
        jnp.concatenate([owns] * 3, axis=1), jnp.concatenate([high, middle, low], axis=0),
        preferred_element_type=jnp.float32)
    parts[...] = summed.reshape(groups, CP_DEV, cc * LANES)
    for i in range(1, groups):
        to = lax.rem(me + i, groups)
        cp = pltpu.make_async_remote_copy(
            src_ref=parts.at[to], dst_ref=rs.at[i], send_sem=rs_send.at[i], recv_sem=rs_recv.at[i],
            device_id={"set": to}, device_id_type=MESH)
        cp.start()
        sends.append(cp)

    for i in range(1, zs):
        pltpu.make_async_remote_copy(
            src_ref=gsend, dst_ref=grecv.at[i], send_sem=g_send.at[i], recv_sem=g_recv.at[i],
            device_id={"path": lax.rem(mz + i, zs)}, device_id_type=MESH).wait_recv()
    eye = (lax.broadcasted_iota(jnp.int32, (NB + 8, LANES), 0) == lax.broadcasted_iota(jnp.int32, (NB + 8, LANES), 1))
    ridge = jnp.where(eye & (lax.broadcasted_iota(jnp.int32, (NB + 8, LANES), 0) < width), 0.001, 0.0)
    fits = []
    for step in range(STEPS):
        gram = gsend[step]
        for i in range(1, zs):
            gram = gram + grecv[i, step]
        inverse = sweep_inverse(gram / total_paths + ridge, width)
        fits.append(jnp.dot(
            inverse[:, : NB + 8], basis[step, : NB + 8, :], precision=HIGH,
            preferred_element_type=jnp.float32) / total_paths)

    netted = parts[me]
    for i in range(1, groups):
        pltpu.make_async_remote_copy(
            src_ref=parts.at[0], dst_ref=rs.at[i], send_sem=rs_send.at[i], recv_sem=rs_recv.at[i],
            device_id={"set": lax.rem(me + i, groups)}, device_id_type=MESH).wait_recv()
        netted = netted + rs[i]
    for step in range(STEPS):
        msend[step] = lax.dot_general(
            netted[:, step * group_paths : (step + 1) * group_paths], basis[step], CONTRACT_LANES, precision=HIGH,
            preferred_element_type=jnp.float32)
    for i in range(1, zs):
        cp = pltpu.make_async_remote_copy(
            src_ref=msend, dst_ref=mrecv.at[i], send_sem=m_send.at[i], recv_sem=m_recv.at[i],
            device_id={"path": lax.rem(mz + i, zs)}, device_id_type=MESH)
        cp.start()
        sends.append(cp)
    for i in range(1, zs):
        pltpu.make_async_remote_copy(
            src_ref=msend, dst_ref=mrecv.at[i], send_sem=m_send.at[i], recv_sem=m_recv.at[i],
            device_id={"path": lax.rem(mz + i, zs)}, device_id_type=MESH).wait_recv()
    for step in range(STEPS):
        moments = msend[step]
        for i in range(1, zs):
            moments = moments + mrecv[i, step]
        fitted = jnp.dot(moments[:, : NB + 8], fits[step], precision=HIGH, preferred_element_type=jnp.float32)
        mine = netted[:, step * group_paths : (step + 1) * group_paths]
        expo_ref[step] = jnp.maximum(mine - 0.9 * fitted, 0.0)

    c_expo = pltpu.make_async_copy(expo_ref, expo_hbm, misc_sem.at[9])
    c_expo.start()

    def sent(c, carry):
        slab_copy(me, c, slab_send.at[0, c], sibling).wait_send()
        for i in range(1, groups // 2):
            slab_copy(me, c, slab_send.at[i, c], sibling).wait_send()
            slab_copy(me, c, slab_fwd.at[i, c], sibling).wait_send()
        return carry

    lax.fori_loop(0, chunks, sent, 0)
    for cp in sends:
        cp.wait_send()
    c_expo.wait()
    c_end.wait()


def hand_on(expo_in, end_in, expo_out, end_out, sem):
    first = pltpu.make_async_copy(expo_in, expo_out, sem.at[0])
    second = pltpu.make_async_copy(end_in, end_out, sem.at[1])
    first.start()
    second.start()
    first.wait()
    second.wait()


def per_device(start_state, shocks, loading, decay, factor_lists, delta, gamma, currency, owner):
    groups = lax.axis_size("set")
    zs = lax.axis_size("path")
    paths_dev, factors = start_state.shape
    sets, depth = factor_lists.shape
    group_paths = paths_dev * groups
    cc = STEPS * group_paths // LANES
    chunks = factors // CHUNK
    hbm = pl.BlockSpec(memory_space=pltpu.HBM)
    f32, bf16 = jnp.float32, jnp.bfloat16
    dma = pltpu.SemaphoreType.DMA
    results = pl.pallas_call(
        functools.partial(kernel, groups, zs, paths_dev * groups * zs),
        out_shape=(
            jax.ShapeDtypeStruct((STEPS, CP_DEV, group_paths), f32),
            jax.ShapeDtypeStruct((paths_dev, factors), f32),
        ),
        in_specs=[hbm] * 9,
        out_specs=(hbm, hbm),
        scratch_shapes=[
            pltpu.VMEM((paths_dev, factors), f32),
            pltpu.VMEM((STEPS * paths_dev, factors), bf16),
            pltpu.VMEM((factors, factors), bf16),
            pltpu.VMEM((1, factors), f32),
            pltpu.SMEM((depth, sets), jnp.int32),
            pltpu.VMEM((depth, sets), bf16),
            pltpu.SMEM((sets,), jnp.int32),
            pltpu.VMEM((1, sets), jnp.int32),
            pltpu.VMEM((depth * depth, sets), bf16),
            pltpu.VMEM((paths_dev, factors), f32),
            pltpu.VMEM((STEPS, CP_DEV, group_paths), f32),
            pltpu.VMEM((groups, STEPS * paths_dev, factors), bf16),
            pltpu.VMEM((factors * cc + 2 * PAD, LANES), f32),
            pltpu.VMEM((sets * depth // 2, 2 * depth), f32),
            pltpu.VMEM((sets, depth), f32),
            pltpu.VMEM((sets // GROUP, GROUP * depth + 16, GROUP * depth), bf16),
            pltpu.VMEM((NB * cc, LANES), f32),
            pltpu.VMEM((2, GROUP, depth * cc, LANES), f32),
            pltpu.VMEM((sets, cc * LANES), f32),
            pltpu.VMEM((STEPS, LANES, group_paths), f32),
            pltpu.VMEM((groups, CP_DEV, cc * LANES), f32),
            pltpu.VMEM((groups, CP_DEV, cc * LANES), f32),
            pltpu.VMEM((STEPS, NB + 8, LANES), f32),
            pltpu.VMEM((zs, STEPS, NB + 8, LANES), f32),
            pltpu.VMEM((STEPS, CP_DEV, LANES), f32),
            pltpu.VMEM((zs, STEPS, CP_DEV, LANES), f32),
            dma((chunks,)),
            dma((10,)),
            dma((groups, chunks)),
            dma((groups, chunks)),
            dma((groups, chunks)),
            dma((groups,)),
            dma((groups,)),
            dma((zs,)),
            dma((zs,)),
            dma((zs,)),
            dma((zs,)),
        ],
        compiler_params=pltpu.CompilerParams(
            collective_id=0, has_side_effects=True, vmem_limit_bytes=60 * 1024 * 1024
        ),
    )(
        start_state,
        shocks.reshape(STEPS * paths_dev, factors),
        loading,
        decay.reshape(1, factors),
        factor_lists.T,
        delta.T,
        jnp.transpose(gamma, (1, 2, 0)).reshape(depth * depth, sets),
        currency,
        owner.reshape(1, sets),
    )
    return pl.pallas_call(
        hand_on,
        out_shape=tuple(jax.ShapeDtypeStruct(r.shape, r.dtype) for r in results),
        in_specs=[hbm, hbm],
        out_specs=(hbm, hbm),
        scratch_shapes=[dma((2,))],
        compiler_params=pltpu.CompilerParams(vmem_limit_bytes=60 * 1024 * 1024),
    )(*results)


def solution(mesh):
    return jax.shard_map(
        per_device,
        mesh=mesh,
        in_specs=(
            P(("path", "set"), None),
            P(None, ("path", "set"), None),
            P(),
            P(),
            P("set", None),
            P("set", None),
            P("set", None, None),
            P("set"),
            P("set"),
        ),
        out_specs=(P(None, "set", "path"), P(("path", "set"), None)),
        check_vma=False,
    )
```

```python
import functools

import jax
import jax.numpy as jnp
from jax import lax
from jax.experimental import pallas as pl
from jax.experimental.pallas import tpu as pltpu
from jax.sharding import PartitionSpec as P

NB = 16
STEPS = 2
CP_DEV = 8
LANES = 128
CHUNK = 512
PAD = 8
GROUP = 8
MESH = pl.DeviceIdType.MESH
HIGH = lax.Precision.HIGHEST
CONTRACT_LANES = (((1,), (1,)), ((), ()))


def sweep_inverse(a, size):
    rows = lax.broadcasted_iota(jnp.int32, a.shape, 0)
    cols = lax.broadcasted_iota(jnp.int32, a.shape, 1)
    for k in range(size):
        row = a[k : k + 1, :]
        col = a[:, k : k + 1]
        inv = 1.0 / a[k : k + 1, k : k + 1]
        scaled = row * inv
        update = a - col * scaled
        update = jnp.where(cols == k, col * inv, update)
        update = jnp.where(rows == k, jnp.where(cols == k, -inv, scaled), update)
        a = update
    return -a


def kernel(
    groups, zs, total_paths,
    start_hbm, shocks_hbm, loading_hbm, decay_hbm, lists_hbm, delta_hbm, gamma_hbm, cur_hbm, owner_hbm,
    expo_ref, end_v,
    start_v, shocks_v, load_v, decay_ref, lists_s, delta_ref, cur_s, owner_ref, gin_v,
    gath, slab_t, gam, dlin, left, rates, xg, vals, basis, parts, rs, gsend, grecv, msend, mrecv,
    load_sem, misc_sem, slab_send, slab_fwd, slab_recv, rs_send, rs_recv, g_send, g_recv, m_send, m_recv,
):
    paths_dev = start_v.shape[0]
    factors = start_v.shape[1]
    depth, sets = lists_s.shape
    group_paths = paths_dev * groups
    pblocks = group_paths // LANES
    cc = STEPS * pblocks
    chunks = factors // CHUNK
    half = depth // 2
    cps = CP_DEV * groups
    width = NB + 1

    me = lax.axis_index("set")
    mz = lax.axis_index("path")
    sibling = me + 1 - 2 * lax.rem(me, 2)

    c_shocks = pltpu.make_async_copy(shocks_hbm, shocks_v, misc_sem.at[0])
    c_start = pltpu.make_async_copy(start_hbm, start_v, misc_sem.at[1])
    c_decay = pltpu.make_async_copy(decay_hbm, decay_ref, misc_sem.at[8])
    c_shocks.start()
    c_start.start()
    c_decay.start()
    c_load = []
    for c in range(chunks):
        cols = pl.ds(c * CHUNK, CHUNK)
        cp = pltpu.make_async_copy(loading_hbm.at[:, cols], load_v.at[:, cols], load_sem.at[c])
        cp.start()
        c_load.append(cp)
    c_gamma = pltpu.make_async_copy(gamma_hbm, gin_v, misc_sem.at[2])
    c_lists = pltpu.make_async_copy(lists_hbm, lists_s, misc_sem.at[3])
    c_cur = pltpu.make_async_copy(cur_hbm, cur_s, misc_sem.at[4])
    c_delta = pltpu.make_async_copy(delta_hbm, delta_ref, misc_sem.at[6])
    c_owner = pltpu.make_async_copy(owner_hbm, owner_ref, misc_sem.at[7])
    c_gamma.start()
    c_delta.start()
    c_lists.start()
    c_cur.start()
    c_owner.start()

    barrier = pltpu.get_barrier_semaphore()
    for i in range(1, groups):
        pl.semaphore_signal(barrier, inc=1, device_id={"set": lax.rem(me + i, groups)}, device_id_type=MESH)
    for i in range(1, zs):
        pl.semaphore_signal(barrier, inc=1, device_id={"path": lax.rem(mz + i, zs)}, device_id_type=MESH)

    def slab_copy(owner, c, send, to):
        spot = gath.at[owner, :, pl.ds(c * CHUNK, CHUNK)]
        return pltpu.make_async_remote_copy(
            src_ref=spot, dst_ref=spot, send_sem=send, recv_sem=slab_recv.at[owner, c],
            device_id={"set": to}, device_id_type=MESH)

    sends = []
    c_shocks.wait()
    c_start.wait()
    c_decay.wait()
    for c in range(chunks):
        cols = pl.ds(c * CHUNK, CHUNK)
        c_load[c].wait()
        moved = jnp.dot(shocks_v[...], load_v[:, cols], preferred_element_type=jnp.float32)
        decay = decay_ref[:, cols]
        first = decay * start_v[:, cols] + moved[:paths_dev]
        second = decay * first + moved[paths_dev:]
        end_v[:, cols] = second
        gath[me, :paths_dev, cols] = first.astype(jnp.bfloat16)
        gath[me, paths_dev:, cols] = second.astype(jnp.bfloat16)
        if c == 0:
            pl.semaphore_wait(barrier, groups - 1 + zs - 1)
        for i in range(1, groups // 2):
            cp = slab_copy(me, c, slab_send.at[i, c], lax.rem(me + 2 * i, groups))
            cp.start()
            sends.append(cp)
        cp = slab_copy(me, c, slab_send.at[0, c], sibling)
        cp.start()
        sends.append(cp)

    def relay(m, carry):
        upper = gin_v[pl.ds(pl.multiple_of(m * depth, depth), depth), :]
        lower = gin_v[pl.ds(pl.multiple_of((m + half) * depth, depth), depth), :]
        both = jnp.concatenate([upper, lower], axis=0).astype(jnp.float32)
        gam[pl.ds(m, sets, stride=half), :] = both.T
        return carry

    def prepare(j, carry):
        pair = gam[pl.ds(pl.multiple_of(j * half, half), half), :]
        linear = jnp.broadcast_to(dlin[pl.ds(j, 1), :], (16, depth))
        left[j] = jnp.concatenate([pair[:, :depth], pair[:, depth:], linear], axis=0).astype(jnp.bfloat16)
        return carry

    def piece(c):
        early = chunks // 2
        if c == 0:
            c_gamma.wait()
            c_delta.wait()
            dlin[...] = delta_ref[...].astype(jnp.float32).T
        if c < early:
            lax.fori_loop(half * c // early, half * (c + 1) // early, relay, 0, unroll=4)
        else:
            at, late = c - early, chunks - early
            lax.fori_loop(sets * at // late, sets * (at + 1) // late, prepare, 0, unroll=8)

    def forward(c):
        for i in range(1, groups // 2):
            src = lax.rem(me + 2 * i, groups)
            slab_copy(src, c, slab_fwd.at[i, c], sibling).wait_recv()
            cp = slab_copy(src, c, slab_fwd.at[i, c], sibling)
            cp.start()
            sends.append(cp)

    def turn(c):
        slab_copy(sibling, c, slab_send.at[0, c], sibling).wait_recv()
        for i in range(1, groups // 2):
            slab_copy(lax.rem(sibling + 2 * i, groups), c, slab_fwd.at[i, c], sibling).wait_recv()
        for step in range(STEPS):
            for b in range(CHUNK // LANES):
                f0 = c * CHUNK + b * LANES
                block = gath[:, step * paths_dev : (step + 1) * paths_dev, f0 : f0 + LANES]
                block = block.reshape(group_paths, LANES).astype(jnp.float32).T
                for q in range(pblocks):
                    slab_t[pl.ds(PAD + f0 * cc + step * pblocks + q, LANES, stride=cc), :] = block[
                        :, q * LANES : (q + 1) * LANES
                    ]

    def send_gram():
        rates[...] = jnp.exp(0.2 * slab_t[PAD : PAD + NB * cc, :])
        basis[...] = jnp.zeros_like(basis)
        for step in range(STEPS):
            for q in range(pblocks):
                basis[step, :NB, q * LANES : (q + 1) * LANES] = slab_t[
                    pl.ds(PAD + step * pblocks + q, NB, stride=cc), :
                ]
            basis[step, NB : NB + 1, :] = jnp.ones((1, group_paths), jnp.float32)
            gsend[step] = lax.dot_general(
                basis[step, : NB + 8, :], basis[step], CONTRACT_LANES, precision=HIGH,
                preferred_element_type=jnp.float32)
        for i in range(1, zs):
            cp = pltpu.make_async_remote_copy(
                src_ref=gsend, dst_ref=grecv.at[i], send_sem=g_send.at[i], recv_sem=g_recv.at[i],
                device_id={"path": lax.rem(mz + i, zs)}, device_id_type=MESH)
            cp.start()
            sends.append(cp)

    for c in range(chunks):
        piece(c)
        forward(c)
        if c > 0:
            turn(c - 1)
        if c == 1:
            send_gram()
    turn(chunks - 1)

    c_lists.wait()
    c_cur.wait()

    merged = max(1, PAD // cc)
    span = merged * cc
    sublane = lax.broadcasted_iota(jnp.int32, (span, LANES), 0)

    def gather(buf, u, j):
        for k in range(0, depth, merged):
            rows = slab_t[pl.ds(lists_s[k, j] * cc + PAD, span), :]
            for r in range(1, merged):
                window = slab_t[pl.ds(lists_s[k + r, j] * cc + (PAD - r * cc), span), :]
                rows = jnp.where(sublane >= r * cc, window, rows)
            xg[buf, u, k * cc : k * cc + span, :] = rows

    def value(buf, u, j):
        x = jnp.concatenate([xg[buf, u, pl.ds(c, depth, stride=cc), :] for c in range(cc)], axis=1)
        prod = jnp.dot(left[j], x.astype(jnp.bfloat16), preferred_element_type=jnp.float32)
        local = prod[depth : depth + 1] + 0.5 * jnp.sum(x * prod[:depth], axis=0, keepdims=True)
        at = cur_s[j] * cc
        return local * jnp.concatenate([rates[pl.ds(at + c, 1), :] for c in range(cc)], axis=1)

    rounds = sets // GROUP

    def revalue(i, carry):
        for buf in range(2):
            g = 2 * i + buf
            later = lax.rem(g + 1, rounds)
            rows = []
            for u in range(GROUP):
                gather(1 - buf, u, later * GROUP + u)
                rows.append(value(buf, u, g * GROUP + u))
            vals[pl.ds(pl.multiple_of(g * GROUP, GROUP), GROUP), :] = jnp.concatenate(rows, axis=0)
        return carry

    for u in range(GROUP):
        gather(0, u, u)
    lax.fori_loop(0, rounds // 2, revalue, 0)

    c_owner.wait()
    owns = lax.broadcasted_iota(jnp.int32, (cps, sets), 0) == owner_ref[...]
    owns = owns.astype(jnp.bfloat16)
    value_f32 = vals[...]
    high = value_f32.astype(jnp.bfloat16)
    rest = value_f32 - high.astype(jnp.float32)
    middle = rest.astype(jnp.bfloat16)
    low = (rest - middle.astype(jnp.float32)).astype(jnp.bfloat16)
    summed = jnp.dot(
        jnp.concatenate([owns] * 3, axis=1), jnp.concatenate([high, middle, low], axis=0),
        preferred_element_type=jnp.float32)
    parts[...] = summed.reshape(groups, CP_DEV, cc * LANES)
    for i in range(1, groups):
        to = lax.rem(me + i, groups)
        cp = pltpu.make_async_remote_copy(
            src_ref=parts.at[to], dst_ref=rs.at[i], send_sem=rs_send.at[i], recv_sem=rs_recv.at[i],
            device_id={"set": to}, device_id_type=MESH)
        cp.start()
        sends.append(cp)

    for i in range(1, zs):
        pltpu.make_async_remote_copy(
            src_ref=gsend, dst_ref=grecv.at[i], send_sem=g_send.at[i], recv_sem=g_recv.at[i],
            device_id={"path": lax.rem(mz + i, zs)}, device_id_type=MESH).wait_recv()
    eye = (lax.broadcasted_iota(jnp.int32, (NB + 8, LANES), 0) == lax.broadcasted_iota(jnp.int32, (NB + 8, LANES), 1))
    ridge = jnp.where(eye & (lax.broadcasted_iota(jnp.int32, (NB + 8, LANES), 0) < width), 0.001, 0.0)
    fits = []
    for step in range(STEPS):
        gram = gsend[step]
        for i in range(1, zs):
            gram = gram + grecv[i, step]
        inverse = sweep_inverse(gram / total_paths + ridge, width)
        fits.append(jnp.dot(
            inverse[:, : NB + 8], basis[step, : NB + 8, :], precision=HIGH,
            preferred_element_type=jnp.float32) / total_paths)

    netted = parts[me]
    for i in range(1, groups):
        pltpu.make_async_remote_copy(
            src_ref=parts.at[0], dst_ref=rs.at[i], send_sem=rs_send.at[i], recv_sem=rs_recv.at[i],
            device_id={"set": lax.rem(me + i, groups)}, device_id_type=MESH).wait_recv()
        netted = netted + rs[i]
    for step in range(STEPS):
        msend[step] = lax.dot_general(
            netted[:, step * group_paths : (step + 1) * group_paths], basis[step], CONTRACT_LANES, precision=HIGH,
            preferred_element_type=jnp.float32)
    for i in range(1, zs):
        cp = pltpu.make_async_remote_copy(
            src_ref=msend, dst_ref=mrecv.at[i], send_sem=m_send.at[i], recv_sem=m_recv.at[i],
            device_id={"path": lax.rem(mz + i, zs)}, device_id_type=MESH)
        cp.start()
        sends.append(cp)
    for i in range(1, zs):
        pltpu.make_async_remote_copy(
            src_ref=msend, dst_ref=mrecv.at[i], send_sem=m_send.at[i], recv_sem=m_recv.at[i],
            device_id={"path": lax.rem(mz + i, zs)}, device_id_type=MESH).wait_recv()
    for step in range(STEPS):
        moments = msend[step]
        for i in range(1, zs):
            moments = moments + mrecv[i, step]
        fitted = jnp.dot(moments[:, : NB + 8], fits[step], precision=HIGH, preferred_element_type=jnp.float32)
        mine = netted[:, step * group_paths : (step + 1) * group_paths]
        expo_ref[step] = jnp.maximum(mine - 0.9 * fitted, 0.0)

    for cp in sends:
        cp.wait_send()


def per_device(start_state, shocks, loading, decay, factor_lists, delta, gamma, currency, owner):
    groups = lax.axis_size("set")
    zs = lax.axis_size("path")
    paths_dev, factors = start_state.shape
    sets, depth = factor_lists.shape
    group_paths = paths_dev * groups
    cc = STEPS * group_paths // LANES
    chunks = factors // CHUNK
    hbm = pl.BlockSpec(memory_space=pltpu.HBM)
    vmem = pl.BlockSpec(memory_space=pltpu.VMEM)
    f32, bf16 = jnp.float32, jnp.bfloat16
    dma = pltpu.SemaphoreType.DMA
    return pl.pallas_call(
        functools.partial(kernel, groups, zs, paths_dev * groups * zs),
        out_shape=(
            pltpu.VMEM((STEPS, CP_DEV, group_paths), f32),
            pltpu.VMEM((paths_dev, factors), f32),
        ),
        in_specs=[hbm] * 9,
        out_specs=(vmem, vmem),
        scratch_shapes=[
            pltpu.VMEM((paths_dev, factors), f32),
            pltpu.VMEM((STEPS * paths_dev, factors), bf16),
            pltpu.VMEM((factors, factors), bf16),
            pltpu.VMEM((1, factors), f32),
            pltpu.SMEM((depth, sets), jnp.int32),
            pltpu.VMEM((depth, sets), bf16),
            pltpu.SMEM((sets,), jnp.int32),
            pltpu.VMEM((1, sets), jnp.int32),
            pltpu.VMEM((depth * depth, sets), bf16),
            pltpu.VMEM((groups, STEPS * paths_dev, factors), bf16),
            pltpu.VMEM((factors * cc + 2 * PAD, LANES), f32),
            pltpu.VMEM((sets * depth // 2, 2 * depth), f32),
            pltpu.VMEM((sets, depth), f32),
            pltpu.VMEM((sets, depth + 16, depth), bf16),
            pltpu.VMEM((NB * cc, LANES), f32),
            pltpu.VMEM((2, GROUP, depth * cc, LANES), f32),
            pltpu.VMEM((sets, cc * LANES), f32),
            pltpu.VMEM((STEPS, LANES, group_paths), f32),
            pltpu.VMEM((groups, CP_DEV, cc * LANES), f32),
            pltpu.VMEM((groups, CP_DEV, cc * LANES), f32),
            pltpu.VMEM((STEPS, NB + 8, LANES), f32),
            pltpu.VMEM((zs, STEPS, NB + 8, LANES), f32),
            pltpu.VMEM((STEPS, CP_DEV, LANES), f32),
            pltpu.VMEM((zs, STEPS, CP_DEV, LANES), f32),
            dma((chunks,)),
            dma((10,)),
            dma((groups, chunks)),
            dma((groups, chunks)),
            dma((groups, chunks)),
            dma((groups,)),
            dma((groups,)),
            dma((zs,)),
            dma((zs,)),
            dma((zs,)),
            dma((zs,)),
        ],
        compiler_params=pltpu.CompilerParams(
            collective_id=0, has_side_effects=True, vmem_limit_bytes=60 * 1024 * 1024
        ),
    )(
        start_state,
        shocks.reshape(STEPS * paths_dev, factors),
        loading,
        decay.reshape(1, factors),
        factor_lists.T,
        delta.T,
        jnp.transpose(gamma, (1, 2, 0)).reshape(depth * depth, sets),
        currency,
        owner.reshape(1, sets),
    )


def solution(mesh):
    return jax.shard_map(
        per_device,
        mesh=mesh,
        in_specs=(
            P(("path", "set"), None),
            P(None, ("path", "set"), None),
            P(),
            P(),
            P("set", None),
            P("set", None),
            P("set", None, None),
            P("set"),
            P("set"),
        ),
        out_specs=(P(None, "set", "path"), P(("path", "set"), None)),
        check_vma=False,
    )
```

```python
import functools

import jax
import jax.numpy as jnp
from jax import lax
from jax.experimental import pallas as pl
from jax.experimental.pallas import tpu as pltpu
from jax.sharding import PartitionSpec as P

NB = 16
STEPS = 2
CP_DEV = 8
LANES = 128
CHUNK = 512
PAD = 8
GROUP = 8
MESH = pl.DeviceIdType.MESH
HIGH = lax.Precision.HIGHEST
CONTRACT_LANES = (((1,), (1,)), ((), ()))


def sweep_inverse(a, size):
    rows = lax.broadcasted_iota(jnp.int32, a.shape, 0)
    cols = lax.broadcasted_iota(jnp.int32, a.shape, 1)
    for k in range(size):
        row = a[k : k + 1, :]
        col = a[:, k : k + 1]
        inv = 1.0 / a[k : k + 1, k : k + 1]
        scaled = row * inv
        update = a - col * scaled
        update = jnp.where(cols == k, col * inv, update)
        update = jnp.where(rows == k, jnp.where(cols == k, -inv, scaled), update)
        a = update
    return -a


def kernel(
    groups, zs, total_paths,
    start_hbm, shocks_hbm, loading_hbm, decay_hbm, lists_hbm, delta_hbm, gamma_hbm, cur_hbm, owner_hbm,
    expo_ref, end_v,
    start_v, shocks_v, load_v, decay_ref, lists_s, delta_ref, cur_s, owner_ref, gin_v,
    gath, slab_t, gam, dlin, left, rates, xg, vals, basis, parts, rs, gsend, grecv, bcat, hcat, mrecv,
    load_sem, misc_sem, slab_send, slab_fwd, slab_recv, rs_send, rs_recv, g_send, g_recv, m_send, m_recv,
):
    paths_dev = start_v.shape[0]
    factors = start_v.shape[1]
    depth, sets = lists_s.shape
    group_paths = paths_dev * groups
    pblocks = group_paths // LANES
    cc = STEPS * pblocks
    chunks = factors // CHUNK
    half = depth // 2
    cps = CP_DEV * groups
    width = NB + 1
    share = LANES // STEPS

    me = lax.axis_index("set")
    mz = lax.axis_index("path")
    sibling = me + 1 - 2 * lax.rem(me, 2)

    c_shocks = pltpu.make_async_copy(shocks_hbm, shocks_v, misc_sem.at[0])
    c_start = pltpu.make_async_copy(start_hbm, start_v, misc_sem.at[1])
    c_decay = pltpu.make_async_copy(decay_hbm, decay_ref, misc_sem.at[8])
    c_shocks.start()
    c_start.start()
    c_decay.start()
    c_load = []
    for c in range(chunks):
        cols = pl.ds(c * CHUNK, CHUNK)
        cp = pltpu.make_async_copy(loading_hbm.at[:, cols], load_v.at[:, cols], load_sem.at[c])
        cp.start()
        c_load.append(cp)
    c_gamma = pltpu.make_async_copy(gamma_hbm, gin_v, misc_sem.at[2])
    c_lists = pltpu.make_async_copy(lists_hbm, lists_s, misc_sem.at[3])
    c_cur = pltpu.make_async_copy(cur_hbm, cur_s, misc_sem.at[4])
    c_delta = pltpu.make_async_copy(delta_hbm, delta_ref, misc_sem.at[6])
    c_owner = pltpu.make_async_copy(owner_hbm, owner_ref, misc_sem.at[7])
    c_gamma.start()
    c_delta.start()
    c_lists.start()
    c_cur.start()
    c_owner.start()

    barrier = pltpu.get_barrier_semaphore()
    others = [(dz, ds) for dz in range(zs) for ds in range(groups) if dz or ds]

    def place(dz, ds):
        return {"path": lax.rem(mz + dz, zs), "set": lax.rem(me + ds, groups)}

    for dz, ds in others:
        pl.semaphore_signal(barrier, inc=1, device_id=place(dz, ds), device_id_type=MESH)

    def slab_copy(owner, c, send, to):
        spot = gath.at[owner, :, pl.ds(c * CHUNK, CHUNK)]
        return pltpu.make_async_remote_copy(
            src_ref=spot, dst_ref=spot, send_sem=send, recv_sem=slab_recv.at[owner, c],
            device_id={"set": to}, device_id_type=MESH)

    sends = []
    c_shocks.wait()
    c_start.wait()
    c_decay.wait()
    for c in range(chunks):
        cols = pl.ds(c * CHUNK, CHUNK)
        c_load[c].wait()
        moved = jnp.dot(shocks_v[...], load_v[:, cols], preferred_element_type=jnp.float32)
        decay = decay_ref[:, cols]
        first = decay * start_v[:, cols] + moved[:paths_dev]
        second = decay * first + moved[paths_dev:]
        end_v[:, cols] = second
        gath[me, :paths_dev, cols] = first.astype(jnp.bfloat16)
        gath[me, paths_dev:, cols] = second.astype(jnp.bfloat16)
        if c == 0:
            pl.semaphore_wait(barrier, len(others))
        for i in range(1, groups // 2):
            cp = slab_copy(me, c, slab_send.at[i, c], lax.rem(me + 2 * i, groups))
            cp.start()
            sends.append(cp)
        cp = slab_copy(me, c, slab_send.at[0, c], sibling)
        cp.start()
        sends.append(cp)

    def relay(m, carry):
        upper = gin_v[pl.ds(pl.multiple_of(m * depth, depth), depth), :]
        lower = gin_v[pl.ds(pl.multiple_of((m + half) * depth, depth), depth), :]
        both = jnp.concatenate([upper, lower], axis=0).astype(jnp.float32)
        gam[pl.ds(m, sets, stride=half), :] = both.T
        return carry

    def prepare(j, carry):
        pair = gam[pl.ds(pl.multiple_of(j * half, half), half), :]
        linear = jnp.broadcast_to(dlin[pl.ds(j, 1), :], (16, depth))
        left[j] = jnp.concatenate([pair[:, :depth], pair[:, depth:], linear], axis=0).astype(jnp.bfloat16)
        return carry

    def piece(c):
        early = chunks // 2
        if c == 0:
            c_gamma.wait()
            c_delta.wait()
            dlin[...] = delta_ref[...].astype(jnp.float32).T
        if c < early:
            lax.fori_loop(half * c // early, half * (c + 1) // early, relay, 0, unroll=4)
        else:
            at, late = c - early, chunks - early
            lax.fori_loop(sets * at // late, sets * (at + 1) // late, prepare, 0, unroll=8)

    def forward(c):
        for i in range(1, groups // 2):
            src = lax.rem(me + 2 * i, groups)
            slab_copy(src, c, slab_fwd.at[i, c], sibling).wait_recv()
            cp = slab_copy(src, c, slab_fwd.at[i, c], sibling)
            cp.start()
            sends.append(cp)

    def turn(c):
        slab_copy(sibling, c, slab_send.at[0, c], sibling).wait_recv()
        for i in range(1, groups // 2):
            slab_copy(lax.rem(sibling + 2 * i, groups), c, slab_fwd.at[i, c], sibling).wait_recv()
        for step in range(STEPS):
            for b in range(CHUNK // LANES):
                f0 = c * CHUNK + b * LANES
                block = gath[:, step * paths_dev : (step + 1) * paths_dev, f0 : f0 + LANES]
                block = block.reshape(group_paths, LANES).astype(jnp.float32).T
                for q in range(pblocks):
                    slab_t[pl.ds(PAD + f0 * cc + step * pblocks + q, LANES, stride=cc), :] = block[
                        :, q * LANES : (q + 1) * LANES
                    ]

    spots = [slice(step * share, step * share + NB + 8) for step in range(STEPS)]
    spans = [slice(step * group_paths, (step + 1) * group_paths) for step in range(STEPS)]

    def send_gram():
        rates[...] = jnp.exp(0.2 * slab_t[PAD : PAD + NB * cc, :])
        basis[...] = jnp.zeros_like(basis)
        bcat[...] = jnp.zeros_like(bcat)
        hcat[...] = jnp.zeros_like(hcat)
        for step in range(STEPS):
            for q in range(pblocks):
                basis[step, :NB, q * LANES : (q + 1) * LANES] = slab_t[
                    pl.ds(PAD + step * pblocks + q, NB, stride=cc), :
                ]
            basis[step, NB : NB + 1, :] = jnp.ones((1, group_paths), jnp.float32)
            bcat[spots[step], spans[step]] = basis[step, : NB + 8, :]
            gsend[step] = lax.dot_general(
                basis[step, : NB + 8, :], basis[step], CONTRACT_LANES, precision=HIGH,
                preferred_element_type=jnp.float32)
        for i in range(1, zs):
            cp = pltpu.make_async_remote_copy(
                src_ref=gsend, dst_ref=grecv.at[i], send_sem=g_send.at[i], recv_sem=g_recv.at[i],
                device_id={"path": lax.rem(mz + i, zs)}, device_id_type=MESH)
            cp.start()
            sends.append(cp)

    for c in range(chunks):
        piece(c)
        forward(c)
        if c > 0:
            turn(c - 1)
        if c == 1:
            send_gram()
    turn(chunks - 1)

    c_lists.wait()
    c_cur.wait()

    merged = max(1, PAD // cc)
    span = merged * cc
    sublane = lax.broadcasted_iota(jnp.int32, (span, LANES), 0)

    def gather(buf, u, j):
        for k in range(0, depth, merged):
            rows = slab_t[pl.ds(lists_s[k, j] * cc + PAD, span), :]
            for r in range(1, merged):
                window = slab_t[pl.ds(lists_s[k + r, j] * cc + (PAD - r * cc), span), :]
                rows = jnp.where(sublane >= r * cc, window, rows)
            xg[buf, u, k * cc : k * cc + span, :] = rows

    def value(buf, u, j):
        x = jnp.concatenate([xg[buf, u, pl.ds(c, depth, stride=cc), :] for c in range(cc)], axis=1)
        prod = jnp.dot(left[j], x.astype(jnp.bfloat16), preferred_element_type=jnp.float32)
        local = prod[depth : depth + 1] + 0.5 * jnp.sum(x * prod[:depth], axis=0, keepdims=True)
        at = cur_s[j] * cc
        return local * jnp.concatenate([rates[pl.ds(at + c, 1), :] for c in range(cc)], axis=1)

    rounds = sets // GROUP

    def revalue(i, carry):
        for buf in range(2):
            g = 2 * i + buf
            later = lax.rem(g + 1, rounds)
            rows = []
            for u in range(GROUP):
                gather(1 - buf, u, later * GROUP + u)
                rows.append(value(buf, u, g * GROUP + u))
            vals[pl.ds(pl.multiple_of(g * GROUP, GROUP), GROUP), :] = jnp.concatenate(rows, axis=0)
        return carry

    for u in range(GROUP):
        gather(0, u, u)
    lax.fori_loop(0, rounds // 2, revalue, 0)

    c_owner.wait()
    owns = lax.broadcasted_iota(jnp.int32, (cps, sets), 0) == owner_ref[...]
    owns = owns.astype(jnp.bfloat16)
    value_f32 = vals[...]
    high = value_f32.astype(jnp.bfloat16)
    rest = value_f32 - high.astype(jnp.float32)
    middle = rest.astype(jnp.bfloat16)
    low = (rest - middle.astype(jnp.float32)).astype(jnp.bfloat16)
    summed = jnp.dot(
        jnp.concatenate([owns] * 3, axis=1), jnp.concatenate([high, middle, low], axis=0),
        preferred_element_type=jnp.float32)
    parts[:, :, : cc * LANES] = summed.reshape(groups, CP_DEV, cc * LANES)
    moments = lax.dot_general(summed, bcat[...], CONTRACT_LANES, precision=HIGH, preferred_element_type=jnp.float32)
    parts[:, :, cc * LANES :] = moments.reshape(groups, CP_DEV, LANES)

    def block_copy(dz, ds):
        to = lax.rem(me + ds, groups)
        if dz:
            slot = dz * groups + ds
            return pltpu.make_async_remote_copy(
                src_ref=parts.at[to, :, pl.ds(cc * LANES, LANES)], dst_ref=mrecv.at[slot], send_sem=m_send.at[slot],
                recv_sem=m_recv.at[slot], device_id=place(dz, ds), device_id_type=MESH)
        return pltpu.make_async_remote_copy(
            src_ref=parts.at[to], dst_ref=rs.at[ds], send_sem=rs_send.at[ds], recv_sem=rs_recv.at[ds],
            device_id=place(dz, ds), device_id_type=MESH)

    for dz, ds in others:
        cp = block_copy(dz, ds)
        cp.start()
        sends.append(cp)

    for i in range(1, zs):
        pltpu.make_async_remote_copy(
            src_ref=gsend, dst_ref=grecv.at[i], send_sem=g_send.at[i], recv_sem=g_recv.at[i],
            device_id={"path": lax.rem(mz + i, zs)}, device_id_type=MESH).wait_recv()
    eye = (lax.broadcasted_iota(jnp.int32, (NB + 8, LANES), 0) == lax.broadcasted_iota(jnp.int32, (NB + 8, LANES), 1))
    ridge = jnp.where(eye & (lax.broadcasted_iota(jnp.int32, (NB + 8, LANES), 0) < width), 0.001, 0.0)
    for step in range(STEPS):
        gram = gsend[step]
        for i in range(1, zs):
            gram = gram + grecv[i, step]
        inverse = sweep_inverse(gram / total_paths + ridge, width)
        hcat[spots[step], spans[step]] = jnp.dot(
            inverse[:, : NB + 8], basis[step, : NB + 8, :], precision=HIGH,
            preferred_element_type=jnp.float32) / total_paths

    total = parts[me]
    for dz, ds in others:
        block_copy(dz, ds).wait_recv()
        if not dz:
            total = total + rs[ds]
    netted = total[:, : cc * LANES]
    moments = total[:, cc * LANES :]
    for dz, ds in others:
        if dz:
            moments = moments + mrecv[dz * groups + ds]
    fitted = jnp.dot(moments, hcat[...], precision=HIGH, preferred_element_type=jnp.float32)
    result = jnp.maximum(netted - 0.9 * fitted, 0.0)
    for step in range(STEPS):
        expo_ref[step] = result[:, spans[step]]

    for cp in sends:
        cp.wait_send()


def per_device(start_state, shocks, loading, decay, factor_lists, delta, gamma, currency, owner):
    groups = lax.axis_size("set")
    zs = lax.axis_size("path")
    paths_dev, factors = start_state.shape
    sets, depth = factor_lists.shape
    group_paths = paths_dev * groups
    cc = STEPS * group_paths // LANES
    chunks = factors // CHUNK
    hbm = pl.BlockSpec(memory_space=pltpu.HBM)
    vmem = pl.BlockSpec(memory_space=pltpu.VMEM)
    f32, bf16 = jnp.float32, jnp.bfloat16
    dma = pltpu.SemaphoreType.DMA
    return pl.pallas_call(
        functools.partial(kernel, groups, zs, paths_dev * groups * zs),
        out_shape=(
            pltpu.VMEM((STEPS, CP_DEV, group_paths), f32),
            pltpu.VMEM((paths_dev, factors), f32),
        ),
        in_specs=[hbm] * 9,
        out_specs=(vmem, vmem),
        scratch_shapes=[
            pltpu.VMEM((paths_dev, factors), f32),
            pltpu.VMEM((STEPS * paths_dev, factors), bf16),
            pltpu.VMEM((factors, factors), bf16),
            pltpu.VMEM((1, factors), f32),
            pltpu.SMEM((depth, sets), jnp.int32),
            pltpu.VMEM((depth, sets), bf16),
            pltpu.SMEM((sets,), jnp.int32),
            pltpu.VMEM((1, sets), jnp.int32),
            pltpu.VMEM((depth * depth, sets), bf16),
            pltpu.VMEM((groups, STEPS * paths_dev, factors), bf16),
            pltpu.VMEM((factors * cc + 2 * PAD, LANES), f32),
            pltpu.VMEM((sets * depth // 2, 2 * depth), f32),
            pltpu.VMEM((sets, depth), f32),
            pltpu.VMEM((sets, depth + 16, depth), bf16),
            pltpu.VMEM((NB * cc, LANES), f32),
            pltpu.VMEM((2, GROUP, depth * cc, LANES), f32),
            pltpu.VMEM((sets, cc * LANES), f32),
            pltpu.VMEM((STEPS, LANES, group_paths), f32),
            pltpu.VMEM((groups, CP_DEV, (cc + 1) * LANES), f32),
            pltpu.VMEM((groups, CP_DEV, (cc + 1) * LANES), f32),
            pltpu.VMEM((STEPS, NB + 8, LANES), f32),
            pltpu.VMEM((zs, STEPS, NB + 8, LANES), f32),
            pltpu.VMEM((LANES, cc * LANES), f32),
            pltpu.VMEM((LANES, cc * LANES), f32),
            pltpu.VMEM((zs * groups, CP_DEV, LANES), f32),
            dma((chunks,)),
            dma((10,)),
            dma((groups, chunks)),
            dma((groups, chunks)),
            dma((groups, chunks)),
            dma((groups,)),
            dma((groups,)),
            dma((zs,)),
            dma((zs,)),
            dma((zs * groups,)),
            dma((zs * groups,)),
        ],
        compiler_params=pltpu.CompilerParams(
            collective_id=0, has_side_effects=True, vmem_limit_bytes=60 * 1024 * 1024
        ),
    )(
        start_state,
        shocks.reshape(STEPS * paths_dev, factors),
        loading,
        decay.reshape(1, factors),
        factor_lists.T,
        delta.T,
        jnp.transpose(gamma, (1, 2, 0)).reshape(depth * depth, sets),
        currency,
        owner.reshape(1, sets),
    )


def solution(mesh):
    return jax.shard_map(
        per_device,
        mesh=mesh,
        in_specs=(
            P(("path", "set"), None),
            P(None, ("path", "set"), None),
            P(),
            P(),
            P("set", None),
            P("set", None),
            P("set", None, None),
            P("set"),
            P("set"),
        ),
        out_specs=(P(None, "set", "path"), P(("path", "set"), None)),
        check_vma=False,
    )
```

```python
import functools

import jax
import jax.numpy as jnp
from jax import lax
from jax.experimental import pallas as pl
from jax.experimental.pallas import tpu as pltpu
from jax.sharding import PartitionSpec as P

NB = 16
STEPS = 2
CP_DEV = 8
LANES = 128
CHUNK = 256
PAD = 8
GROUP = 8
MESH = pl.DeviceIdType.MESH
HIGH = lax.Precision.HIGHEST
CONTRACT_LANES = (((1,), (1,)), ((), ()))


def sweep_inverse(a, size):
    rows = lax.broadcasted_iota(jnp.int32, a.shape, 0)
    cols = lax.broadcasted_iota(jnp.int32, a.shape, 1)
    for k in range(size):
        row = a[k : k + 1, :]
        col = a[:, k : k + 1]
        inv = 1.0 / a[k : k + 1, k : k + 1]
        scaled = row * inv
        update = a - col * scaled
        update = jnp.where(cols == k, col * inv, update)
        update = jnp.where(rows == k, jnp.where(cols == k, -inv, scaled), update)
        a = update
    return -a


def kernel(
    groups, zs, total_paths,
    start_hbm, shocks_hbm, loading_hbm, decay_hbm, lists_hbm, delta_hbm, gamma_hbm, cur_hbm, owner_hbm,
    expo_ref, end_v,
    start_v, shocks_v, load_v, decay_ref, lists_s, delta_ref, cur_s, owner_ref, gin_v,
    gath, slab_t, gam, dlin, left, rates, xg, vals, basis, parts, rs, gsend, grecv, bcat, hcat, mrecv,
    load_sem, misc_sem, slab_send, slab_fwd, slab_recv, rs_send, rs_recv, g_send, g_recv, m_send, m_recv,
):
    paths_dev = start_v.shape[0]
    factors = start_v.shape[1]
    depth, sets = lists_s.shape
    group_paths = paths_dev * groups
    pblocks = group_paths // LANES
    cc = STEPS * pblocks
    chunks = factors // CHUNK
    half = depth // 2
    cps = CP_DEV * groups
    width = NB + 1
    share = LANES // STEPS

    me = lax.axis_index("set")
    mz = lax.axis_index("path")
    sibling = me + 1 - 2 * lax.rem(me, 2)

    c_shocks = pltpu.make_async_copy(shocks_hbm, shocks_v, misc_sem.at[0])
    c_start = pltpu.make_async_copy(start_hbm, start_v, misc_sem.at[1])
    c_decay = pltpu.make_async_copy(decay_hbm, decay_ref, misc_sem.at[8])
    c_shocks.start()
    c_start.start()
    c_decay.start()
    c_load = []
    for c in range(chunks):
        cols = pl.ds(c * CHUNK, CHUNK)
        cp = pltpu.make_async_copy(loading_hbm.at[:, cols], load_v.at[:, cols], load_sem.at[c])
        cp.start()
        c_load.append(cp)
    c_gamma = pltpu.make_async_copy(gamma_hbm, gin_v, misc_sem.at[2])
    c_lists = pltpu.make_async_copy(lists_hbm, lists_s, misc_sem.at[3])
    c_cur = pltpu.make_async_copy(cur_hbm, cur_s, misc_sem.at[4])
    c_delta = pltpu.make_async_copy(delta_hbm, delta_ref, misc_sem.at[6])
    c_owner = pltpu.make_async_copy(owner_hbm, owner_ref, misc_sem.at[7])
    c_gamma.start()
    c_delta.start()
    c_lists.start()
    c_cur.start()
    c_owner.start()

    barrier = pltpu.get_barrier_semaphore()
    others = [(dz, ds) for dz in range(zs) for ds in range(groups) if dz or ds]

    def place(dz, ds):
        return {"path": lax.rem(mz + dz, zs), "set": lax.rem(me + ds, groups)}

    for dz, ds in others:
        pl.semaphore_signal(barrier, inc=1, device_id=place(dz, ds), device_id_type=MESH)

    def slab_copy(owner, c, send, to):
        spot = gath.at[owner, :, pl.ds(c * CHUNK, CHUNK)]
        return pltpu.make_async_remote_copy(
            src_ref=spot, dst_ref=spot, send_sem=send, recv_sem=slab_recv.at[owner, c],
            device_id={"set": to}, device_id_type=MESH)

    sends = []
    c_shocks.wait()
    c_start.wait()
    c_decay.wait()
    for c in range(chunks):
        cols = pl.ds(c * CHUNK, CHUNK)
        c_load[c].wait()
        moved = jnp.dot(shocks_v[...], load_v[:, cols], preferred_element_type=jnp.float32)
        decay = decay_ref[:, cols]
        first = decay * start_v[:, cols] + moved[:paths_dev]
        second = decay * first + moved[paths_dev:]
        end_v[:, cols] = second
        gath[me, :paths_dev, cols] = first.astype(jnp.bfloat16)
        gath[me, paths_dev:, cols] = second.astype(jnp.bfloat16)
        if c == 0:
            pl.semaphore_wait(barrier, len(others))
        for i in range(1, groups // 2):
            cp = slab_copy(me, c, slab_send.at[i, c], lax.rem(me + 2 * i, groups))
            cp.start()
            sends.append(cp)
        cp = slab_copy(me, c, slab_send.at[0, c], sibling)
        cp.start()
        sends.append(cp)

    def relay(m, carry):
        upper = gin_v[pl.ds(pl.multiple_of(m * depth, depth), depth), :]
        lower = gin_v[pl.ds(pl.multiple_of((m + half) * depth, depth), depth), :]
        both = jnp.concatenate([upper, lower], axis=0).astype(jnp.float32)
        gam[pl.ds(m, sets, stride=half), :] = both.T
        return carry

    def prepare(j, carry):
        pair = gam[pl.ds(pl.multiple_of(j * half, half), half), :]
        linear = jnp.broadcast_to(dlin[pl.ds(j, 1), :], (16, depth))
        left[j] = jnp.concatenate([pair[:, :depth], pair[:, depth:], linear], axis=0).astype(jnp.bfloat16)
        return carry

    def piece(c):
        early = chunks // 2
        if c == 0:
            c_gamma.wait()
            c_delta.wait()
            dlin[...] = delta_ref[...].astype(jnp.float32).T
        if c < early:
            lax.fori_loop(half * c // early, half * (c + 1) // early, relay, 0, unroll=4)
        else:
            at, late = c - early, chunks - early
            lax.fori_loop(sets * at // late, sets * (at + 1) // late, prepare, 0, unroll=8)

    def forward(c):
        for i in range(1, groups // 2):
            src = lax.rem(me + 2 * i, groups)
            slab_copy(src, c, slab_fwd.at[i, c], sibling).wait_recv()
            cp = slab_copy(src, c, slab_fwd.at[i, c], sibling)
            cp.start()
            sends.append(cp)

    def turn(c):
        slab_copy(sibling, c, slab_send.at[0, c], sibling).wait_recv()
        for i in range(1, groups // 2):
            slab_copy(lax.rem(sibling + 2 * i, groups), c, slab_fwd.at[i, c], sibling).wait_recv()
        for step in range(STEPS):
            for b in range(CHUNK // LANES):
                f0 = c * CHUNK + b * LANES
                block = gath[:, step * paths_dev : (step + 1) * paths_dev, f0 : f0 + LANES]
                block = block.reshape(group_paths, LANES).astype(jnp.float32).T
                for q in range(pblocks):
                    slab_t[pl.ds(PAD + f0 * cc + step * pblocks + q, LANES, stride=cc), :] = block[
                        :, q * LANES : (q + 1) * LANES
                    ]

    spots = [slice(step * share, step * share + NB + 8) for step in range(STEPS)]
    spans = [slice(step * group_paths, (step + 1) * group_paths) for step in range(STEPS)]

    def send_gram():
        rates[...] = jnp.exp(0.2 * slab_t[PAD : PAD + NB * cc, :])
        basis[...] = jnp.zeros_like(basis)
        bcat[...] = jnp.zeros_like(bcat)
        hcat[...] = jnp.zeros_like(hcat)
        for step in range(STEPS):
            for q in range(pblocks):
                basis[step, :NB, q * LANES : (q + 1) * LANES] = slab_t[
                    pl.ds(PAD + step * pblocks + q, NB, stride=cc), :
                ]
            basis[step, NB : NB + 1, :] = jnp.ones((1, group_paths), jnp.float32)
            bcat[spots[step], spans[step]] = basis[step, : NB + 8, :]
            gsend[step] = lax.dot_general(
                basis[step, : NB + 8, :], basis[step], CONTRACT_LANES, precision=HIGH,
                preferred_element_type=jnp.float32)
        for i in range(1, zs):
            cp = pltpu.make_async_remote_copy(
                src_ref=gsend, dst_ref=grecv.at[i], send_sem=g_send.at[i], recv_sem=g_recv.at[i],
                device_id={"path": lax.rem(mz + i, zs)}, device_id_type=MESH)
            cp.start()
            sends.append(cp)

    for c in range(chunks):
        piece(c)
        forward(c)
        if c > 0:
            turn(c - 1)
        if c == 1:
            send_gram()
    turn(chunks - 1)

    c_lists.wait()
    c_cur.wait()

    merged = max(1, PAD // cc)
    span = merged * cc
    sublane = lax.broadcasted_iota(jnp.int32, (span, LANES), 0)

    def gather(buf, u, j):
        for k in range(0, depth, merged):
            rows = slab_t[pl.ds(lists_s[k, j] * cc + PAD, span), :]
            for r in range(1, merged):
                window = slab_t[pl.ds(lists_s[k + r, j] * cc + (PAD - r * cc), span), :]
                rows = jnp.where(sublane >= r * cc, window, rows)
            xg[buf, u, k * cc : k * cc + span, :] = rows

    def value(buf, u, j):
        x = jnp.concatenate([xg[buf, u, pl.ds(c, depth, stride=cc), :] for c in range(cc)], axis=1)
        prod = jnp.dot(left[j], x.astype(jnp.bfloat16), preferred_element_type=jnp.float32)
        local = prod[depth : depth + 1] + 0.5 * jnp.sum(x * prod[:depth], axis=0, keepdims=True)
        at = cur_s[j] * cc
        return local * jnp.concatenate([rates[pl.ds(at + c, 1), :] for c in range(cc)], axis=1)

    rounds = sets // GROUP

    def revalue(i, carry):
        for buf in range(2):
            g = 2 * i + buf
            later = lax.rem(g + 1, rounds)
            rows = []
            for u in range(GROUP):
                gather(1 - buf, u, later * GROUP + u)
                rows.append(value(buf, u, g * GROUP + u))
            vals[pl.ds(pl.multiple_of(g * GROUP, GROUP), GROUP), :] = jnp.concatenate(rows, axis=0)
        return carry

    for u in range(GROUP):
        gather(0, u, u)
    lax.fori_loop(0, rounds // 2, revalue, 0)

    c_owner.wait()
    owns = lax.broadcasted_iota(jnp.int32, (cps, sets), 0) == owner_ref[...]
    owns = owns.astype(jnp.bfloat16)
    value_f32 = vals[...]
    high = value_f32.astype(jnp.bfloat16)
    rest = value_f32 - high.astype(jnp.float32)
    middle = rest.astype(jnp.bfloat16)
    low = (rest - middle.astype(jnp.float32)).astype(jnp.bfloat16)
    summed = jnp.dot(
        jnp.concatenate([owns] * 3, axis=1), jnp.concatenate([high, middle, low], axis=0),
        preferred_element_type=jnp.float32)
    parts[:, :, : cc * LANES] = summed.reshape(groups, CP_DEV, cc * LANES)
    moments = lax.dot_general(summed, bcat[...], CONTRACT_LANES, precision=HIGH, preferred_element_type=jnp.float32)
    parts[:, :, cc * LANES :] = moments.reshape(groups, CP_DEV, LANES)

    def block_copy(dz, ds):
        to = lax.rem(me + ds, groups)
        if dz:
            slot = dz * groups + ds
            return pltpu.make_async_remote_copy(
                src_ref=parts.at[to, :, pl.ds(cc * LANES, LANES)], dst_ref=mrecv.at[slot], send_sem=m_send.at[slot],
                recv_sem=m_recv.at[slot], device_id=place(dz, ds), device_id_type=MESH)
        return pltpu.make_async_remote_copy(
            src_ref=parts.at[to], dst_ref=rs.at[ds], send_sem=rs_send.at[ds], recv_sem=rs_recv.at[ds],
            device_id=place(dz, ds), device_id_type=MESH)

    for dz, ds in others:
        cp = block_copy(dz, ds)
        cp.start()
        sends.append(cp)

    for i in range(1, zs):
        pltpu.make_async_remote_copy(
            src_ref=gsend, dst_ref=grecv.at[i], send_sem=g_send.at[i], recv_sem=g_recv.at[i],
            device_id={"path": lax.rem(mz + i, zs)}, device_id_type=MESH).wait_recv()
    eye = (lax.broadcasted_iota(jnp.int32, (NB + 8, LANES), 0) == lax.broadcasted_iota(jnp.int32, (NB + 8, LANES), 1))
    ridge = jnp.where(eye & (lax.broadcasted_iota(jnp.int32, (NB + 8, LANES), 0) < width), 0.001, 0.0)
    for step in range(STEPS):
        gram = gsend[step]
        for i in range(1, zs):
            gram = gram + grecv[i, step]
        inverse = sweep_inverse(gram / total_paths + ridge, width)
        hcat[spots[step], spans[step]] = jnp.dot(
            inverse[:, : NB + 8], basis[step, : NB + 8, :], precision=HIGH,
            preferred_element_type=jnp.float32) / total_paths

    total = parts[me]
    for dz, ds in others:
        block_copy(dz, ds).wait_recv()
        if not dz:
            total = total + rs[ds]
    netted = total[:, : cc * LANES]
    moments = total[:, cc * LANES :]
    for dz, ds in others:
        if dz:
            moments = moments + mrecv[dz * groups + ds]
    fitted = jnp.dot(moments, hcat[...], precision=HIGH, preferred_element_type=jnp.float32)
    result = jnp.maximum(netted - 0.9 * fitted, 0.0)
    for step in range(STEPS):
        expo_ref[step] = result[:, spans[step]]

    for cp in sends:
        cp.wait_send()


def per_device(start_state, shocks, loading, decay, factor_lists, delta, gamma, currency, owner):
    groups = lax.axis_size("set")
    zs = lax.axis_size("path")
    paths_dev, factors = start_state.shape
    sets, depth = factor_lists.shape
    group_paths = paths_dev * groups
    cc = STEPS * group_paths // LANES
    chunks = factors // CHUNK
    hbm = pl.BlockSpec(memory_space=pltpu.HBM)
    vmem = pl.BlockSpec(memory_space=pltpu.VMEM)
    f32, bf16 = jnp.float32, jnp.bfloat16
    dma = pltpu.SemaphoreType.DMA
    return pl.pallas_call(
        functools.partial(kernel, groups, zs, paths_dev * groups * zs),
        out_shape=(
            pltpu.VMEM((STEPS, CP_DEV, group_paths), f32),
            pltpu.VMEM((paths_dev, factors), f32),
        ),
        in_specs=[hbm] * 9,
        out_specs=(vmem, vmem),
        scratch_shapes=[
            pltpu.VMEM((paths_dev, factors), f32),
            pltpu.VMEM((STEPS * paths_dev, factors), bf16),
            pltpu.VMEM((factors, factors), bf16),
            pltpu.VMEM((1, factors), f32),
            pltpu.SMEM((depth, sets), jnp.int32),
            pltpu.VMEM((depth, sets), bf16),
            pltpu.SMEM((sets,), jnp.int32),
            pltpu.VMEM((1, sets), jnp.int32),
            pltpu.VMEM((depth * depth, sets), bf16),
            pltpu.VMEM((groups, STEPS * paths_dev, factors), bf16),
            pltpu.VMEM((factors * cc + 2 * PAD, LANES), f32),
            pltpu.VMEM((sets * depth // 2, 2 * depth), f32),
            pltpu.VMEM((sets, depth), f32),
            pltpu.VMEM((sets, depth + 16, depth), bf16),
            pltpu.VMEM((NB * cc, LANES), f32),
            pltpu.VMEM((2, GROUP, depth * cc, LANES), f32),
            pltpu.VMEM((sets, cc * LANES), f32),
            pltpu.VMEM((STEPS, LANES, group_paths), f32),
            pltpu.VMEM((groups, CP_DEV, (cc + 1) * LANES), f32),
            pltpu.VMEM((groups, CP_DEV, (cc + 1) * LANES), f32),
            pltpu.VMEM((STEPS, NB + 8, LANES), f32),
            pltpu.VMEM((zs, STEPS, NB + 8, LANES), f32),
            pltpu.VMEM((LANES, cc * LANES), f32),
            pltpu.VMEM((LANES, cc * LANES), f32),
            pltpu.VMEM((zs * groups, CP_DEV, LANES), f32),
            dma((chunks,)),
            dma((10,)),
            dma((groups, chunks)),
            dma((groups, chunks)),
            dma((groups, chunks)),
            dma((groups,)),
            dma((groups,)),
            dma((zs,)),
            dma((zs,)),
            dma((zs * groups,)),
            dma((zs * groups,)),
        ],
        compiler_params=pltpu.CompilerParams(
            collective_id=0, has_side_effects=True, vmem_limit_bytes=60 * 1024 * 1024
        ),
    )(
        start_state,
        shocks.reshape(STEPS * paths_dev, factors),
        loading,
        decay.reshape(1, factors),
        factor_lists.T,
        delta.T,
        jnp.transpose(gamma, (1, 2, 0)).reshape(depth * depth, sets),
        currency,
        owner.reshape(1, sets),
    )


def solution(mesh):
    return jax.shard_map(
        per_device,
        mesh=mesh,
        in_specs=(
            P(("path", "set"), None),
            P(None, ("path", "set"), None),
            P(),
            P(),
            P("set", None),
            P("set", None),
            P("set", None, None),
            P("set"),
            P("set"),
        ),
        out_specs=(P(None, "set", "path"), P(("path", "set"), None)),
        check_vma=False,
    )
```
